256 devices in a mesh: seq: 128 (over y, z, x_lo, core), head: 2 (over x_hi).
Axes of the slice: x: 4 (x_hi: 2, x_lo: 2; x = x_hi * 2 + x_lo), y: 4, z: 8, core: 2. Of those that a mesh axis runs over, the one named last changes fastest.
Arguments:
- queries: bfloat16 [16384, 4096], P('seq', 'head'), may hold values from -36 to 36
- keys: bfloat16 [16384, 1024], P('seq', 'head'), may hold values from -7.5 to 7.5
- values: bfloat16 [16384, 1024], P('seq', 'head'), may hold values from -16 to 16
- windows: int32 [32], P('head'), may hold values from 64 to 256, as said below
- out_weight: bfloat16 [4096, 4096], P('head', 'seq'), may hold values from -0.09375 to 0.09375
- grad_out: bfloat16 [16384, 4096], P('seq', 'head'), may hold values from -6 to 6
Outputs:
- output: bfloat16 [16384, 4096], P('seq', 'head')
- grad_queries: bfloat16 [16384, 4096], P('seq', 'head')
- grad_keys: bfloat16 [16384, 1024], P('seq', 'head')
- grad_values: bfloat16 [16384, 1024], P('seq', 'head')
The draws below stay inside these ranges and needn't reach their ends.
Inputs may be any that keep to these rules, and one draw needn't show every extreme that they name: windows[h] counts the latest positions, the query's own included, that query head h attends besides the first 4 tokens.
All inputs are finite; a program needn't handle non-finite values.
Results may differ from the reference program's by a relative error of at most 0.034.
Values may be sent and summed in bfloat16 or wider, within the bound.
A program may use at most 64 MiB of HBM per device.

```python
import math
import jax
import jax.numpy as jnp
from jax import lax

D = 4096
Q_HEADS = 32
KV_HEADS = 8
HEAD_DIM = 128
SINKS = 4
SLAB = 128
TOKENS = 16384


def paired_draws(key):
    group_size = Q_HEADS // KV_HEADS
    key_shape = (TOKENS, KV_HEADS, HEAD_DIM)
    query_shape = (TOKENS, KV_HEADS, group_size, HEAD_DIM)
    base_keys = jnp.clip(jax.random.normal(jax.random.fold_in(key, 11), key_shape, jnp.float32), -5.0, 5.0)
    base_queries = jnp.clip(jax.random.normal(jax.random.fold_in(key, 12), query_shape, jnp.float32), -5.0, 5.0)
    return (base_queries.reshape(TOKENS, Q_HEADS * HEAD_DIM), base_keys.reshape(TOKENS, KV_HEADS * HEAD_DIM))


def draw_queries(key, part):
    return paired_draws(key)[0].astype(jnp.bfloat16)


def draw_keys(key, part):
    return paired_draws(key)[1].astype(jnp.bfloat16)


def draw_windows(key, part):
    spans = jax.random.randint(jax.random.fold_in(key, 21), (Q_HEADS,), SLAB // 2, 2 * SLAB + 1)
    order = jax.random.permutation(jax.random.fold_in(key, 22), Q_HEADS)
    spans = jnp.where(order == 0, 2 * SLAB, spans)
    spans = jnp.where(order == 1, SLAB // 2, spans)
    return spans.astype(jnp.int32)


def shard_levels(own_key, shape, split, least, top_value):
    factor_of = 1.0
    for dim, shards_of in split:
        steps = jax.random.uniform(jax.random.fold_in(jax.random.fold_in(own_key, 6), dim), (shards_of,), jnp.float32, least / len(split), top_value / len(split))
        factor_of = factor_of * jnp.repeat(jnp.exp(steps), shape[dim] // shards_of).reshape((-1,) + (1,) * (len(shape) - 1 - dim))
    return factor_of


def centred(own_key, extent, scale, most, cuts=(), kind=jnp.bfloat16):
    entries = scale * jax.random.normal(own_key, extent, jnp.float32)
    if cuts:
        entries = entries * shard_levels(own_key, extent, cuts, -0.22, 0.18)
    return jnp.clip(entries, -most, most).astype(kind)


def setup_inputs(seed: int = 0) -> dict:
    key_of = jax.random.split(jax.random.key(seed), 7)
    return {
        "queries": draw_queries(jax.random.fold_in(key_of[6], 71), 0),
        "keys": draw_keys(jax.random.fold_in(key_of[6], 71), 0),
        "values": centred(key_of[2], (TOKENS, KV_HEADS * HEAD_DIM), 4.0, 16.0, ((0, 128), (1, 2))),
        "windows": draw_windows(jax.random.fold_in(key_of[6], 71), 0),
        "out_weight": centred(key_of[4], (Q_HEADS * HEAD_DIM, D), (Q_HEADS * HEAD_DIM) ** -0.5, 0.09375, ((0, 2), (1, 128))),
        "grad_out": centred(key_of[5], (TOKENS, D), 1.0, 6.0, ((0, 128), (1, 2))),
    }


MASKED_SCORE = -1e+30

def split_heads(array, row_count):
    return array.reshape(row_count, KV_HEADS, HEAD_DIM).transpose(1, 0, 2)

def merge_heads(array):
    return array.transpose(1, 0, 2).reshape(array.shape[1], -1)

def head_masks(head_windows, positions):
    query_pos, key_pos, sink_pos = positions
    distance = query_pos[:, None] - key_pos[None, :]
    inside = (distance >= 0) & (key_pos[None, :] >= SINKS)
    in_window = distance[None] < head_windows[:, None, None]
    band_mask = inside[None] & in_window
    sink_mask = (sink_pos[None, :] <= query_pos[:, None])[None]
    return (band_mask, sink_mask)

def head_scores(query_heads, band_keys, sink_keys, band_mask, sink_mask):
    score_scale = 1.0 / math.sqrt(HEAD_DIM)
    query_f = query_heads.astype(jnp.float32)
    band_scores = jnp.einsum('gtd,jd->gtj', query_f, band_keys.astype(jnp.float32)) * score_scale
    sink_scores = jnp.einsum('gtd,sd->gts', query_f, sink_keys.astype(jnp.float32)) * score_scale
    return (jnp.where(band_mask, band_scores, MASKED_SCORE), jnp.where(sink_mask, sink_scores, MASKED_SCORE))

def forward_head(query_heads, band_keys, band_values, sink_keys, sink_values, head_windows, positions):
    band_mask, sink_mask = head_masks(head_windows, positions)
    band_scores, sink_scores = head_scores(query_heads, band_keys, sink_keys, band_mask, sink_mask)
    row_max = jnp.maximum(band_scores.max(-1), sink_scores.max(-1))
    totals = jnp.exp(band_scores - row_max[..., None]).sum(-1) + jnp.exp(sink_scores - row_max[..., None]).sum(-1)
    log_total = row_max + jnp.log(totals)
    band_probs = jnp.where(band_mask, jnp.exp(band_scores - log_total[..., None]), 0.0).astype(jnp.bfloat16)
    sink_probs = jnp.where(sink_mask, jnp.exp(sink_scores - log_total[..., None]), 0.0).astype(jnp.bfloat16)
    attn = jnp.einsum('gtj,jd->gtd', band_probs.astype(jnp.float32), band_values.astype(jnp.float32))
    attn = attn + jnp.einsum('gts,sd->gtd', sink_probs.astype(jnp.float32), sink_values.astype(jnp.float32))
    return (attn.astype(jnp.bfloat16), log_total)

def backward_head(query_heads, band_keys, band_values, sink_keys, sink_values, head_windows, log_total, attn_head, grad_head, positions):
    band_mask, sink_mask = head_masks(head_windows, positions)
    band_scores, sink_scores = head_scores(query_heads, band_keys, sink_keys, band_mask, sink_mask)
    band_probs = jnp.where(band_mask, jnp.exp(band_scores - log_total[..., None]), 0.0)
    sink_probs = jnp.where(sink_mask, jnp.exp(sink_scores - log_total[..., None]), 0.0)
    grad_f = grad_head.astype(jnp.float32)
    delta = lax.optimization_barrier(jnp.sum(grad_f * attn_head.astype(jnp.float32), -1))
    band_dprobs = jnp.einsum('gtd,jd->gtj', grad_f, band_values.astype(jnp.float32))
    sink_dprobs = jnp.einsum('gtd,sd->gts', grad_f, sink_values.astype(jnp.float32))
    score_scale = 1.0 / math.sqrt(HEAD_DIM)
    band_dscores = (band_probs * (band_dprobs - delta[..., None]) * score_scale).astype(jnp.bfloat16).astype(jnp.float32)
    sink_dscores = (sink_probs * (sink_dprobs - delta[..., None]) * score_scale).astype(jnp.bfloat16).astype(jnp.float32)
    grad_query = jnp.einsum('gtj,jd->gtd', band_dscores, band_keys.astype(jnp.float32))
    grad_query = grad_query + jnp.einsum('gts,sd->gtd', sink_dscores, sink_keys.astype(jnp.float32))
    query_f = query_heads.astype(jnp.float32)
    band_low = band_probs.astype(jnp.bfloat16).astype(jnp.float32)
    sink_low = sink_probs.astype(jnp.bfloat16).astype(jnp.float32)
    band_key_grads = jnp.einsum('gtj,gtd->jd', band_dscores, query_f)
    band_value_grads = jnp.einsum('gtj,gtd->jd', band_low, grad_f)
    sink_key_grads = jnp.einsum('gts,gtd->sd', sink_dscores, query_f)
    sink_value_grads = jnp.einsum('gts,gtd->sd', sink_low, grad_f)
    return (grad_query.astype(jnp.bfloat16), band_key_grads, band_value_grads, sink_key_grads, sink_value_grads)

def reference(queries, keys, values, windows, out_weight, grad_out):
    tokens = queries.shape[0]
    slab_count = tokens // SLAB
    group_size = Q_HEADS // KV_HEADS
    kv_width = KV_HEADS * HEAD_DIM
    pad_rows = jnp.zeros((2 * SLAB, kv_width), keys.dtype)
    padded_keys = jnp.concatenate([pad_rows, keys], 0)
    padded_values = jnp.concatenate([pad_rows, values], 0)
    sink_keys = split_heads(keys[:SINKS], SINKS)
    sink_values = split_heads(values[:SINKS], SINKS)
    head_windows = windows.reshape(KV_HEADS, group_size)
    forward_all = jax.vmap(forward_head, in_axes=(0, 0, 0, 0, 0, 0, None))
    backward_all = jax.vmap(backward_head, in_axes=(0, 0, 0, 0, 0, 0, 0, 0, 0, None))

    def to_heads(array):
        return array.reshape(SLAB, KV_HEADS, group_size, HEAD_DIM).transpose(1, 2, 0, 3)

    def from_heads(array):
        return array.transpose(2, 0, 1, 3).reshape(SLAB, Q_HEADS * HEAD_DIM)

    def slab_inputs(slab_index):
        first_row = (slab_index * SLAB).astype(jnp.int32)
        query_heads = to_heads(lax.dynamic_slice_in_dim(queries, first_row, SLAB, 0))
        band_keys = split_heads(lax.dynamic_slice_in_dim(padded_keys, first_row, 3 * SLAB, 0), 3 * SLAB)
        band_values = split_heads(lax.dynamic_slice_in_dim(padded_values, first_row, 3 * SLAB, 0), 3 * SLAB)
        band_start = first_row - 2 * SLAB
        positions = (first_row + jnp.arange(SLAB, dtype=jnp.int32), band_start + jnp.arange(3 * SLAB, dtype=jnp.int32), jnp.arange(SINKS, dtype=jnp.int32))
        return (first_row, query_heads, band_keys, band_values, positions)

    def forward_slab(slab_index):
        first_row, query_heads, band_keys, band_values, positions = slab_inputs(slab_index)
        attn_heads, log_total = forward_all(query_heads, band_keys, band_values, sink_keys, sink_values, head_windows, positions)
        return from_heads(attn_heads)
    slab_ids = jnp.arange(slab_count, dtype=jnp.int32)
    attn = lax.map(forward_slab, slab_ids).reshape(tokens, Q_HEADS * HEAD_DIM)
    output = jnp.dot(attn, out_weight, preferred_element_type=jnp.float32).astype(jnp.bfloat16)
    grad_attn = jnp.dot(grad_out, out_weight.T, preferred_element_type=jnp.float32).astype(jnp.bfloat16)

    def backward_step(carry, slab_index):
        band_sums, sink_sums = carry
        first_row, query_heads, band_keys, band_values, positions = slab_inputs(slab_index)
        attn_heads, log_total = forward_all(query_heads, band_keys, band_values, sink_keys, sink_values, head_windows, positions)
        grad_heads = to_heads(lax.dynamic_slice_in_dim(grad_attn, first_row, SLAB, 0))
        grad_query, band_key_grads, band_value_grads, sink_key_grads, sink_value_grads = backward_all(query_heads, band_keys, band_values, sink_keys, sink_values, head_windows, log_total, attn_heads, grad_heads, positions)
        merged = jnp.stack([merge_heads(band_key_grads), merge_heads(band_value_grads)])
        current = lax.dynamic_slice_in_dim(band_sums, first_row, 3 * SLAB, 1)
        band_sums = lax.dynamic_update_slice_in_dim(band_sums, current + merged, first_row, 1)
        sink_sums = sink_sums + jnp.stack([merge_heads(sink_key_grads), merge_heads(sink_value_grads)])
        return ((band_sums, sink_sums), from_heads(grad_query))
    start_sums = (jnp.zeros((2, tokens + 2 * SLAB, kv_width), jnp.float32), jnp.zeros((2, SINKS, kv_width), jnp.float32))
    (band_sums, sink_sums), grad_slabs = lax.scan(backward_step, start_sums, slab_ids)
    totals = band_sums[:, 2 * SLAB:]
    totals = totals.at[:, :SINKS].add(sink_sums)
    grad_queries = grad_slabs.reshape(tokens, Q_HEADS * HEAD_DIM)
    return (output, grad_queries, totals[0].astype(jnp.bfloat16), totals[1].astype(jnp.bfloat16))
```

```python
import functools
import math

import jax
import jax.numpy as jnp
from jax import lax
from jax.experimental import pallas as pl
from jax.experimental.pallas import tpu as pltpu
from jax.sharding import PartitionSpec as P

HEAD = 128
SINKS = 4
SLAB = 128
NY, NZ = 4, 8
MASKED = -1e30
FAR_AWAY = 1 << 20
MESH = pl.DeviceIdType.MESH
SCALE = 1.0 / math.sqrt(HEAD)
EXP2_SCALE = SCALE * math.log2(math.e)
Y_FIRST = (256, 256, 256, 128)
STAGES = 4


def dot(a, b, ca, cb):
    return lax.dot_general(a, b, (((ca,), (cb,)), ((), ())), preferred_element_type=jnp.float32)


class Links:
    def __init__(self, send_sems, recv_sems):
        self.send_sems, self.recv_sems = send_sems, recv_sems
        self.copies, self.arrived = {}, set()

    def start(self, name, src, dst, device):
        n = len(self.copies)
        copy = pltpu.make_async_remote_copy(
            src_ref=src,
            dst_ref=dst,
            send_sem=self.send_sems.at[n],
            recv_sem=self.recv_sems.at[n],
            device_id=device,
            device_id_type=MESH,
        )
        copy.start()
        self.copies[name] = copy

    def need(self, *names):
        for name in names:
            if name not in self.arrived:
                self.arrived.add(name)
                self.copies[name].wait_recv()

    def finish(self):
        self.need(*self.copies)
        for copy in self.copies.values():
            copy.wait_send()


def kernel(
    q_ref, k_ref, v_ref, win_ref, w_ref, go_ref,
    out_ref, gq_ref, gk_ref, gv_ref,
    G, kv, go_other, dist, probs, attn, ga, acc, out_send, out_recv, ds_buf, pl_buf, own,
    g_send, g_recv, sinks, sink_r1, sink_r2, sink_r3,
    send_sems, recv_sems, local_sems, tree_send, tree_recv,
):
    s, hd = lax.axis_index("seq"), lax.axis_index("head")
    c, x, z, y = s % 2, (s // 2) % 2, (s // 4) % NZ, s // (4 * NZ)
    n_seq = 4 * NY * NZ

    def at(y, z, x, c):
        return (((y * NZ + z) * 2 + x) * 2 + c, hd)

    def ym(k):
        return (y + k + NY) % NY

    def zm(k):
        return (z + k + NZ) % NZ

    y_dev = {k: at(ym(k), z, x, c) for k in (1, -1, 2)}
    z_dev = {k: at(y, zm(k), x, c) for k in (1, -1)}
    x_dev, sib, pair = at(y, z, 1 - x, c), at(y, z, x, 1 - c), (s, 1 - hd)
    after1, after2 = ((s + 1) % n_seq, hd), ((s + 2) % n_seq, hd)
    before1, before2 = ((s + n_seq - 1) % n_seq, hd), ((s + n_seq - 2) % n_seq, hd)
    quad = 2 * x + c
    leader = quad == 0
    column_leader = leader & (z == 0)
    root = column_leader & (y == 0)

    barrier = pltpu.get_barrier_semaphore()

    def hello(device):
        pl.semaphore_signal(barrier, inc=1, device_id=device, device_id_type=MESH)

    everyone = [y_dev[1], y_dev[-1], y_dev[2], z_dev[1], z_dev[-1], x_dev, sib, pair,
                after1, after2, before1, before2]
    for device in everyone:
        hello(device)

    @pl.when(leader)
    def _():
        for k in range(1, 4):
            hello(at(y, z, k // 2, k % 2))

    @pl.when(column_leader)
    def _():
        for k in range(1, NZ):
            hello(at(y, k, 0, 0))

    @pl.when(root)
    def _():
        for k in range(1, NY):
            hello(at(k, 0, 0, 0))

    @pl.when(quad != 0)
    def _():
        hello(at(y, z, 0, 0))

    @pl.when(leader & (z != 0))
    def _():
        hello(at(y, 0, 0, 0))

    @pl.when(column_leader & (y != 0))
    def _():
        hello(at(0, 0, 0, 0))

    tree_peers = jnp.where(quad != 0, 1, 3 + jnp.where(z != 0, 1, NZ - 1 + jnp.where(y != 0, 1, NY - 1)))
    pl.semaphore_wait(barrier, len(everyone) + tree_peers)

    links = Links(send_sems, recv_sems)
    start, need = links.start, links.need

    locals_ = []
    for h in range(STAGES):
        piece = w_ref.at[:, pl.ds(h * 512, 512)]
        mine = G.at[h, y, z, x, c]
        copy = pltpu.make_async_copy(piece, mine, local_sems.at[h])
        copy.start()
        locals_.append(copy)
        start(("x", h), piece, mine, x_dev)

    kv[0, 2 * SLAB : 3 * SLAB, :] = k_ref[...]
    kv[1, 2 * SLAB : 3 * SLAB, :] = v_ref[...]
    kv[:, 3 * SLAB + 16 :, :] = jnp.zeros((2, SLAB - 16, 512), jnp.bfloat16)
    own_kv = kv.at[:, pl.ds(2 * SLAB, SLAB)]
    first16 = kv.at[:, pl.ds(2 * SLAB, 16)]
    sink_kv = kv.at[:, pl.ds(3 * SLAB, 16)]

    def tree_copy(src, slot, rslot, device):
        return pltpu.make_async_remote_copy(
            src_ref=src, dst_ref=sink_kv, send_sem=tree_send.at[slot], recv_sem=tree_recv.at[rslot],
            device_id=device, device_id_type=MESH)

    def spread():
        @pl.when(root)
        def _():
            kv[:, 3 * SLAB : 3 * SLAB + 16, :] = kv[:, 2 * SLAB : 2 * SLAB + 16, :]
            for k in range(1, NY):
                tree_copy(first16, k, 0, at(k, 0, 0, 0)).start()

        @pl.when(column_leader & (y != 0))
        def _():
            tree_copy(first16, 0, 0, sib).wait_recv()

        @pl.when(column_leader)
        def _():
            for k in range(1, NZ):
                tree_copy(sink_kv, 3 + k, 0, at(y, k, 0, 0)).start()

        @pl.when(leader & (z != 0))
        def _():
            tree_copy(first16, 0, 0, sib).wait_recv()

        @pl.when(leader)
        def _():
            for k in range(1, 4):
                tree_copy(sink_kv, 10 + k, 0, at(y, z, k // 2, k % 2)).start()

        @pl.when(quad != 0)
        def _():
            tree_copy(first16, 0, 0, sib).wait_recv()

        @pl.when(leader)
        def _():
            for k in range(1, 4):
                tree_copy(sink_kv, 10 + k, 0, at(y, z, k // 2, k % 2)).wait_send()

        @pl.when(column_leader)
        def _():
            for k in range(1, NZ):
                tree_copy(sink_kv, 3 + k, 0, at(y, k, 0, 0)).wait_send()

        @pl.when(root)
        def _():
            for k in range(1, NY):
                tree_copy(first16, k, 0, at(k, 0, 0, 0)).wait_send()

    start("near", own_kv, kv.at[:, pl.ds(SLAB, SLAB)], after1)
    start("far", own_kv, kv.at[:, pl.ds(0, SLAB)], after2)
    start("go", go_ref, go_other, pair)

    def lanes(h, first):
        return pl.ds(0, Y_FIRST[h]) if first else pl.ds(Y_FIRST[h], 512 - Y_FIRST[h])

    def block(h, first, ys, zs, xs=pl.ds(0, 2)):
        return G.at[h, ys, zs, xs, c, :, lanes(h, first)]

    one = lambda i: pl.ds(i, 1)
    all_y, all_z = pl.ds(0, NY), pl.ds(0, NZ)
    z_half = {1: pl.ds(0, NZ // 2), -1: pl.ds(NZ // 2, NZ // 2)}
    y_half = {1: pl.ds(0, NY // 2), -1: pl.ds(NY // 2, NY // 2)}

    def push(name, ref, device):
        start(name, ref, ref, device)

    def Ay(h):
        locals_[h].wait()
        need(("x", h))
        for k in (1, -1, 2):
            push(("Ay", h, k), block(h, True, one(y), one(z)), y_dev[k])

    def Az(h, k):
        if k == 1:
            need(*[("Ay", h, j) for j in (1, -1, 2)])
            push(("sA0", h), block(h, True, all_y, one(z)), sib)
        for d in (1, -1):
            ref = block(h, True, all_y, one(zm(-d * (k - 1))))
            if k > 1:
                need(("Az", h, k - 1, d))
                push(("sAz", h, k - 1, d), ref, sib)
            if k == 4:
                ref = block(h, True, y_half[d], one(zm(-d * 3)))
            push(("Az", h, k, d), ref, z_dev[d])

    def Aend(h):
        need(("Az", h, 4, 1), ("Az", h, 4, -1))
        push(("sA4", h), block(h, True, all_y, one(zm(4))), sib)

    def Bz(h, k):
        for d in (1, -1):
            if k > 1:
                need(("Bz", h, k - 1, d))
            xs = pl.ds(0, 2) if k < 4 else pl.ds(0 if d == 1 else 1, 1)
            push(("Bz", h, k, d), block(h, False, one(y), one(zm(-d * (k - 1))), xs), z_dev[d])

    def By(h):
        need(("Bz", h, 4, 1), ("Bz", h, 4, -1))
        for which in (1, -1):
            for d in (1, -1):
                push(("By", h, d, which), block(h, False, one(y), z_half[d * which]), y_dev[d])
        push(("sB0", h), block(h, False, one(y), all_z), sib)

    def By2(h):
        for d in (1, -1):
            need(("By", h, d, 1))
            ref = block(h, False, one(ym(-d)), z_half[d])
            push(("By2", h, d), ref, y_dev[d])
            push(("sBy", h, d, 1), ref, sib)

    def Bend(h):
        for d in (1, -1):
            need(("By", h, d, -1))
            push(("sBy", h, d, -1), block(h, False, one(ym(-d)), z_half[-d]), sib)
        need(("By2", h, 1), ("By2", h, -1))
        push(("sB2", h), block(h, False, one(ym(2)), all_z), sib)

    def gathered(h):
        names = [("sA0", h), ("sA4", h), ("sB0", h), ("sB2", h)]
        names += [("sAz", h, k, d) for k in (1, 2, 3) for d in (1, -1)]
        names += [("sBy", h, d, w) for d in (1, -1) for w in (1, -1)]
        need(*names)

    def masks():
        row = lax.broadcasted_iota(jnp.int32, (SLAB, 4 * SLAB), 0)
        col = lax.broadcasted_iota(jnp.int32, (SLAB, 4 * SLAB), 1)
        first = s * SLAB
        gap = row - col + 2 * SLAB
        band = (col < 3 * SLAB) & (gap >= 0) & (first - 2 * SLAB + col >= SINKS)
        place = col - 3 * SLAB
        sink = (place >= 0) & (place < SINKS) & (place <= first + row)
        dist[...] = jnp.where(band, gap, jnp.where(sink, 0, FAR_AWAY))

    def forward(h):
        keys, vals = kv[0, :, h * HEAD : (h + 1) * HEAD], kv[1, :, h * HEAD : (h + 1) * HEAD]
        for j in range(4 * h, 4 * h + 4):
            cols = slice(j * HEAD, (j + 1) * HEAD)
            scores = dot(q_ref[:, cols], keys, 1, 1)
            scores = jnp.where(dist[...] < win_ref[j], scores, MASKED)
            top = jnp.max(scores, axis=1, keepdims=True)
            p = jnp.exp2((scores - top) * EXP2_SCALE)
            p = p * (1.0 / jnp.sum(p, axis=1, keepdims=True))
            probs[j] = p
            attn[:, cols] = dot(p.astype(jnp.bfloat16), vals, 1, 0).astype(jnp.bfloat16)

    def project(h, half):
        rows = slice(h * 512, (h + 1) * 512)
        for k in range(4):
            yy = 2 * (hd if half == 0 else 1 - hd) + k // 2
            w = G[h, yy, (k % 2) * 4 : (k % 2) * 4 + 4].reshape(512, 512)
            cols = slice(k * 512, (k + 1) * 512)
            o = dot(attn[:, rows], w, 1, 1)
            if h > 0:
                o = o + acc[half, :, cols]
            if h == STAGES - 1 and half == 1:
                out_send[k] = o.astype(jnp.bfloat16)
                start(("out", k), out_send.at[k], out_recv.at[k], pair)
            else:
                acc[half, :, cols] = o
            g = dot((go_ref if half == 0 else go_other)[:, cols], w, 1, 0)
            if half == 1 and k == 0:
                ga[...] = g
            else:
                ga[...] += g

    def backward(h):
        keys, vals = kv[0, :, h * HEAD : (h + 1) * HEAD], kv[1, :, h * HEAD : (h + 1) * HEAD]
        for i in range(4):
            j = 4 * h + i
            cols = slice(j * HEAD, (j + 1) * HEAD)
            g = ga[:, i * HEAD : (i + 1) * HEAD].astype(jnp.bfloat16)
            delta = jnp.sum(
                g.astype(jnp.float32) * attn[:, cols].astype(jnp.float32), axis=1, keepdims=True
            )
            p = probs[j]
            ds = (p * (dot(g, vals, 1, 1) - delta) * SCALE).astype(jnp.bfloat16)
            gq_ref[:, cols] = dot(ds, keys, 1, 0).astype(jnp.bfloat16)
            ds_buf[i * SLAB : (i + 1) * SLAB, :] = ds
            pl_buf[i * SLAB : (i + 1) * SLAB, :] = p.astype(jnp.bfloat16)
        g4 = jnp.concatenate([ga[:, i * HEAD : (i + 1) * HEAD] for i in range(4)], axis=0)
        q4 = jnp.concatenate(
            [q_ref[:, (4 * h + i) * HEAD : (4 * h + i + 1) * HEAD] for i in range(4)], axis=0
        )
        lane = slice(h * HEAD, (h + 1) * HEAD)
        dk = dot(ds_buf[...], q4, 0, 0)
        dv = dot(pl_buf[...], g4.astype(jnp.bfloat16), 0, 0)
        for i, d in enumerate((dk, dv)):
            g_send[h, 0, i] = d[:SLAB].astype(jnp.bfloat16)
            g_send[h, 1, i] = d[SLAB : 2 * SLAB].astype(jnp.bfloat16)
            own[i, :, lane] = d[2 * SLAB : 3 * SLAB]
            sinks[i * 8 : i * 8 + 8, lane] = d[3 * SLAB : 3 * SLAB + 8]
        start(("gfar", h), g_send.at[h, 0], g_recv.at[h, 0], before2)
        start(("gnear", h), g_send.at[h, 1], g_recv.at[h, 1], before1)

    def up(dst, sem, slot, device):
        return pltpu.make_async_remote_copy(
            src_ref=sinks, dst_ref=dst, send_sem=tree_send.at[14], recv_sem=tree_recv.at[sem + slot],
            device_id=device, device_id_type=MESH)

    def collect():
        @pl.when(quad != 0)
        def _():
            copy = up(sink_r1.at[quad - 1], 1, quad - 1, at(y, z, 0, 0))
            copy.start()
            copy.wait_send()

        @pl.when(leader)
        def _():
            for k in range(3):
                up(sink_r1.at[k], 1, k, sib).wait_recv()
            sinks[...] = sinks[...] + sink_r1[0] + sink_r1[1] + sink_r1[2]

            @pl.when(z != 0)
            def _():
                copy = up(sink_r2.at[z - 1], 4, z - 1, at(y, 0, 0, 0))
                copy.start()
                copy.wait_send()

            @pl.when(z == 0)
            def _():
                total = sinks[...]
                for k in range(NZ - 1):
                    up(sink_r2.at[k], 4, k, sib).wait_recv()
                    total = total + sink_r2[k]
                sinks[...] = total

                @pl.when(y != 0)
                def _():
                    copy = up(sink_r3.at[y - 1], 11, y - 1, at(0, 0, 0, 0))
                    copy.start()
                    copy.wait_send()

                @pl.when(y == 0)
                def _():
                    total = sinks[...]
                    for k in range(NY - 1):
                        up(sink_r3.at[k], 11, k, sib).wait_recv()
                        total = total + sink_r3[k]
                    keep = lax.broadcasted_iota(jnp.int32, (8, 512), 0) < SINKS
                    for i in range(2):
                        own[i, 0:8, :] = own[i, 0:8, :] + jnp.where(
                            keep, total[i * 8 : i * 8 + 8], 0.0
                        )

    Ay(0)
    Bz(0, 1)
    Ay(1)
    masks()
    spread()
    Bz(0, 2)
    Az(0, 1)
    Bz(1, 1)
    need("near", "far")
    Bz(0, 3)
    Az(0, 2)
    Bz(1, 2)
    forward(0)
    Bz(0, 4)
    Az(0, 3)
    Bz(1, 3)
    forward(1)
    By(0)
    Az(0, 4)
    Bz(1, 4)
    forward(2)
    Aend(0)
    Az(1, 1)
    Ay(2)
    By2(0)
    By(1)
    forward(3)
    Bz(2, 1)
    Az(1, 2)
    Bend(0)
    need("go")
    Bz(2, 2)
    Az(1, 3)
    gathered(0)
    project(0, 1)
    Bz(2, 3)
    Az(1, 4)
    By2(1)
    project(0, 0)
    Ay(3)
    Bz(2, 4)
    Aend(1)
    Az(2, 1)
    backward(0)
    By(2)
    Bend(1)
    Az(2, 2)
    Bz(3, 1)
    gathered(1)
    project(1, 1)
    Az(2, 3)
    Bz(3, 2)
    project(1, 0)
    By2(2)
    Az(2, 4)
    Bz(3, 3)
    backward(1)
    Aend(2)
    Az(3, 1)
    Bz(3, 4)
    By(3)
    Bend(2)
    Az(3, 2)
    gathered(2)
    project(2, 1)
    Az(3, 3)
    By2(3)
    project(2, 0)
    Az(3, 4)
    backward(2)
    Aend(3)
    Bend(3)
    gathered(3)
    project(3, 1)
    project(3, 0)
    backward(3)
    collect()
    for h in range(STAGES):
        need(("gnear", h), ("gfar", h))
        lane = slice(h * HEAD, (h + 1) * HEAD)
        for i, ref in enumerate((gk_ref, gv_ref)):
            total = own[i, :, lane] + g_recv[h, 0, i].astype(jnp.float32)
            ref[:, lane] = (total + g_recv[h, 1, i].astype(jnp.float32)).astype(jnp.bfloat16)
    for k in range(4):
        cols = slice(k * 512, (k + 1) * 512)
        need(("out", k))
        out_ref[:, cols] = (acc[0, :, cols] + out_recv[k].astype(jnp.float32)).astype(jnp.bfloat16)
    links.finish()


def local(queries, keys, values, windows, out_weight, grad_out):
    vmem = pl.BlockSpec(memory_space=pltpu.VMEM)
    bf, f32 = jnp.bfloat16, jnp.float32
    n_copies = 200
    return pl.pallas_call(
        kernel,
        out_shape=(
            jax.ShapeDtypeStruct((SLAB, 2048), bf),
            jax.ShapeDtypeStruct((SLAB, 2048), bf),
            jax.ShapeDtypeStruct((SLAB, 512), bf),
            jax.ShapeDtypeStruct((SLAB, 512), bf),
        ),
        in_specs=[vmem, vmem, vmem, pl.BlockSpec(memory_space=pltpu.SMEM), vmem, vmem],
        out_specs=(vmem,) * 4,
        scratch_shapes=[
            pltpu.VMEM((STAGES, NY, NZ, 2, 2, 32, 512), bf),
            pltpu.VMEM((2, 4 * SLAB, 512), bf),
            pltpu.VMEM((SLAB, 2048), bf),
            pltpu.VMEM((SLAB, 4 * SLAB), jnp.int32),
            pltpu.VMEM((16, SLAB, 4 * SLAB), f32),
            pltpu.VMEM((SLAB, 2048), bf),
            pltpu.VMEM((SLAB, 512), f32),
            pltpu.VMEM((2, SLAB, 2048), f32),
            pltpu.VMEM((4, SLAB, 512), bf),
            pltpu.VMEM((4, SLAB, 512), bf),
            pltpu.VMEM((4 * SLAB, 4 * SLAB), bf),
            pltpu.VMEM((4 * SLAB, 4 * SLAB), bf),
            pltpu.VMEM((2, SLAB, 512), f32),
            pltpu.VMEM((STAGES, 2, 2, SLAB, HEAD), bf),
            pltpu.VMEM((STAGES, 2, 2, SLAB, HEAD), bf),
            pltpu.VMEM((16, 512), f32),
            pltpu.VMEM((3, 16, 512), f32),
            pltpu.VMEM((NZ - 1, 16, 512), f32),
            pltpu.VMEM((NY - 1, 16, 512), f32),
            pltpu.SemaphoreType.DMA((n_copies,)),
            pltpu.SemaphoreType.DMA((n_copies,)),
            pltpu.SemaphoreType.DMA((STAGES,)),
            pltpu.SemaphoreType.DMA((15,)),
            pltpu.SemaphoreType.DMA((15,)),
        ],
        compiler_params=pltpu.CompilerParams(
            collective_id=0, has_side_effects=True, vmem_limit_bytes=58 << 20
        ),
    )(queries, keys, values, windows, out_weight.T, grad_out)


def solution(mesh):
    cut = P("seq", "head")
    in_specs = (cut, cut, cut, P("head"), P("head", "seq"), cut)
    return jax.shard_map(
        local, mesh=mesh, in_specs=in_specs, out_specs=(cut,) * 4, check_vma=False
    )
```

```python
import functools
import math

import jax
import jax.numpy as jnp
from jax import lax
from jax.experimental import pallas as pl
from jax.experimental.pallas import tpu as pltpu
from jax.sharding import PartitionSpec as P

HEAD = 128
SINKS = 4
SLAB = 128
NY, NZ = 4, 8
MASKED = -1e30
FAR_AWAY = 1 << 20
MESH = pl.DeviceIdType.MESH
SCALE = 1.0 / math.sqrt(HEAD)
EXP2_SCALE = SCALE * math.log2(math.e)
Y_FIRST = (256, 128, 128, 512)
STAGES = 4

ORDER = [
    ("x", 0), ("x", 1), ("x", 2), ("x", 3), ("near",), ("far",), ("go", 0), ("go", 1), ("go", 2), ("go", 3),
    ("Ay", 0, 1), ("Ay", 0, -1), ("Ay", 0, 2), ("Bz", 0, 1, 1), ("Bz", 0, 1, -1), ("By", 0, 1, 0),
    ("By", 0, -1, 0), ("Bz", 1, 1, 1), ("Bz", 1, 1, -1), ("Ay", 1, 1), ("Ay", 1, -1), ("Ay", 1, 2),
    ("By", 1, 1, 0), ("By", 1, -1, 0), ("Bz", 2, 1, 1), ("Bz", 2, 1, -1), ("Ay", 2, 1), ("Ay", 2, -1),
    ("Ay", 2, 2), ("S", 1), ("By", 2, 1, 0), ("By", 2, -1, 0), ("Ay", 3, 1), ("Ay", 3, 2), ("Ay", 3, -1),
    ("Bz", 0, 2, 1), ("Bz", 0, 2, -1), ("Bz", 1, 2, 1), ("Bz", 1, 2, -1), ("sA0", 0), ("Az", 0, 1, 1, None),
    ("By", 0, -1, -1), ("Az", 0, 1, -1, None), ("By", 0, -1, 1), ("Bz", 2, 2, 1), ("Bz", 2, 2, -1), ("S", 2),
    ("sA0", 1), ("Az", 1, 1, 1, None), ("Az", 1, 1, -1, None), ("By", 0, 1, 1), ("By", 1, -1, -1),
    ("By", 0, 1, -1), ("Bz", 0, 3, 1), ("Bz", 0, 3, -1), ("By", 0, -1, -2), ("By", 0, 1, 2), ("Bz", 1, 3, 1),
    ("Bz", 1, 3, -1), ("By", 0, -1, 2), ("sA0", 2), ("By", 0, 1, -2), ("By", 1, -1, -2),
    ("Az", 2, 1, 1, None), ("By2", 0, 1, 0), ("Az", 2, 1, -1, None), ("S", 3), ("F", 0), ("sAz", 0, 1, 1),
    ("sAz", 0, 1, -1), ("By2", 0, -1, -1), ("Az", 0, 2, 1, None), ("Az", 0, 2, -1, None), ("By", 1, 1, 1),
    ("By", 1, 1, -1), ("By", 1, -1, 1), ("By", 1, -1, 2), ("sA0", 3), ("F", 1), ("By2", 0, 1, 1),
    ("sAz", 1, 1, 1), ("Bz", 0, 4, 1), ("Bz", 0, 4, -1), ("By", 0, -1, -3), ("By", 0, 1, 3), ("By", 0, 1, -3),
    ("By", 0, -1, 3), ("By2", 0, 1, 2), ("By2", 0, -1, -2), ("sAz", 1, 1, -1), ("Az", 1, 2, 1, None),
    ("Az", 1, 2, -1, None), ("F", 2), ("Bz", 1, 4, 1), ("Bz", 1, 4, -1), ("By", 1, 1, 2), ("By", 1, 1, -2),
    ("By", 1, -1, -3), ("By", 1, -1, 3), ("Bz", 2, 3, 1), ("Bz", 2, 3, -1), ("sAz", 2, 1, 1),
    ("sAz", 2, 1, -1), ("Az", 2, 2, 1, None), ("By", 1, 1, 3), ("By2", 1, -1, -1), ("Az", 2, 2, -1, None),
    ("F", 3), ("By", 1, 1, -3), ("By2", 1, -1, -2), ("sAz", 0, 2, 1), ("sAz", 0, 2, -1), ("By2", 0, 1, 3),
    ("By2", 0, -1, -3), ("Az", 0, 3, 1, None), ("sB0", 0), ("Az", 0, 3, -1, None), ("By", 0, 1, 4),
    ("By", 0, -1, 4), ("By2", 1, 1, 0), ("By", 2, -1, -1), ("sAz", 1, 2, 1), ("sAz", 1, 2, -1),
    ("Az", 1, 3, 1, None), ("Az", 1, 3, -1, None), ("sB0", 1), ("By", 1, 1, 4), ("By", 1, -1, 4),
    ("Bz", 2, 4, 1), ("Bz", 2, 4, -1), ("By2", 1, 1, 1), ("By2", 1, -1, -3), ("Az", 3, 1, 1, 0),
    ("Az", 3, 1, -1, 0), ("sAz", 2, 2, 1), ("By2", 1, 1, 2), ("sAz", 2, 2, -1), ("By", 2, -1, -2),
    ("Az", 2, 3, 1, None), ("Az", 2, 3, -1, None), ("By2", 1, 1, 3), ("By", 2, -1, 1), ("Az", 3, 1, 1, 1),
    ("By", 2, 1, 1), ("By", 2, -1, -3), ("sBy", 0, 1), ("sBy", 0, -1), ("Az", 3, 1, -1, 1), ("sAz", 0, 3, 1),
    ("sAz", 0, 3, -1), ("By", 2, 1, -1), ("By2", 0, -1, 4), ("Az", 0, 4, 1, None), ("Az", 0, 4, -1, None),
    ("By", 2, -1, 2), ("sAz", 1, 3, 1), ("sAz", 1, 3, -1), ("By", 2, 1, 2), ("sBy", 1, 1), ("sBy", 1, -1),
    ("sB0", 2), ("Az", 1, 4, 1, None), ("Az", 1, 4, -1, None), ("By2", 1, -1, 4), ("By", 2, 1, -2),
    ("Az", 3, 1, 1, 2), ("Az", 3, 1, -1, 2), ("By", 2, -1, 4), ("By", 2, 1, 3), ("Az", 3, 1, 1, 3),
    ("Az", 3, 1, -1, 3), ("By", 2, -1, 3), ("By", 2, 1, -3), ("sAz", 2, 3, 1), ("sAz", 2, 3, -1),
    ("By2", 2, -1, -1), ("Az", 2, 4, 1, None), ("By", 2, 1, 4), ("Az", 2, 4, -1, None), ("Az", 3, 2, 1, 0),
    ("Az", 3, 2, -1, 0), ("By2", 2, -1, -2), ("sB2", 0), ("By2", 2, 1, 0), ("By2", 2, -1, -3), ("sA4", 0),
    ("Az", 3, 2, 1, 1), ("By2", 2, 1, 1), ("Az", 3, 2, -1, 1), ("sA4", 1), ("sB2", 1), ("By2", 2, 1, 2),
    ("Az", 3, 2, 1, 2), ("Az", 3, 2, -1, 2), ("By2", 2, -1, 4), ("PJ", 0), ("By2", 2, 1, 3), ("sBy", 2, -1),
    ("sAz", 3, 1, 1), ("sA4", 2), ("sAz", 3, 1, -1), ("Az", 3, 2, 1, 3), ("Az", 3, 2, -1, 3), ("sBy", 2, 1),
    ("BW", 0), ("Az", 3, 3, 1, 0), ("Az", 3, 3, -1, 0), ("PJ", 1), ("Az", 3, 3, 1, 1), ("Az", 3, 3, -1, 1),
    ("BW", 1), ("Az", 3, 3, 1, 2), ("Az", 3, 3, -1, 2), ("sB2", 2), ("sAz", 3, 2, 1), ("sAz", 3, 2, -1),
    ("Az", 3, 3, 1, 3), ("Az", 3, 3, -1, 3), ("Az", 3, 4, 1, 0), ("PJ", 2), ("Az", 3, 4, 1, 1), ("BW", 2),
    ("Az", 3, 4, -1, 2), ("PZ", 3, 0, 1), ("PZ", 3, 1, 1), ("PZ", 3, 1, -1), ("PZ", 3, 2, 1),
    ("sAz", 3, 3, 1), ("sAz", 3, 3, -1), ("Az", 3, 4, -1, 3), ("PZ", 3, 2, -1), ("PZ", 3, 3, 1),
    ("PZ", 3, 3, -1), ("sA4", 3), ("PZ", 3, 4, 1), ("BW", 3),
]


def dot(a, b, ca, cb):
    return lax.dot_general(a, b, (((ca,), (cb,)), ((), ())), preferred_element_type=jnp.float32)


class Links:
    def __init__(self, send_sems, recv_sems):
        self.send_sems, self.recv_sems = send_sems, recv_sems
        self.copies, self.arrived = {}, set()

    def start(self, name, src, dst, device):
        n = len(self.copies)
        copy = pltpu.make_async_remote_copy(
            src_ref=src,
            dst_ref=dst,
            send_sem=self.send_sems.at[n],
            recv_sem=self.recv_sems.at[n],
            device_id=device,
            device_id_type=MESH,
        )
        copy.start()
        self.copies[name] = copy

    def need(self, *names):
        for name in names:
            if name not in self.arrived:
                self.arrived.add(name)
                self.copies[name].wait_recv()

    def finish(self):
        self.need(*self.copies)
        for copy in self.copies.values():
            copy.wait_send()


def kernel(
    q_ref, k_ref, v_ref, win_ref, w_ref, go_ref,
    out_ref, gq_ref, gk_ref, gv_ref,
    G, kv, go_other, dist, probs, attn, ga, acc, out_send, out_recv, ds_buf, pl_buf, own,
    g_send, g_recv, sinks, sink_r1, sink_r2,
    send_sems, recv_sems, local_sems, tree_send, tree_recv,
):
    s, hd = lax.axis_index("seq"), lax.axis_index("head")
    c, x, z, y = s % 2, (s // 2) % 2, (s // 4) % NZ, s // (4 * NZ)
    n_seq = 4 * NY * NZ

    def at(y, z, x, c):
        return (((y * NZ + z) * 2 + x) * 2 + c, hd)

    def ym(k):
        return (y + k + NY) % NY

    def zm(k):
        return (z + k + NZ) % NZ

    y_dev = {k: at(ym(k), z, x, c) for k in (1, -1, 2)}
    z_dev = {k: at(y, zm(k), x, c) for k in (1, -1)}
    x_dev, sib, pair = at(y, z, 1 - x, c), at(y, z, x, 1 - c), (s, 1 - hd)
    after1, after2 = ((s + 1) % n_seq, hd), ((s + 2) % n_seq, hd)
    before1, before2 = ((s + n_seq - 1) % n_seq, hd), ((s + n_seq - 2) % n_seq, hd)
    quad = 2 * x + c
    leader = quad == 0
    column_leader = leader & (z == 0)
    place = y * NZ + z
    root = column_leader & (y == 0)

    barrier = pltpu.get_barrier_semaphore()

    def hello(device):
        pl.semaphore_signal(barrier, inc=1, device_id=device, device_id_type=MESH)

    everyone = [y_dev[1], y_dev[-1], y_dev[2], z_dev[1], z_dev[-1], x_dev, sib, pair,
                after1, after2, before1, before2]
    for device in everyone:
        hello(device)

    @pl.when(leader)
    def _():
        for k in range(1, 4):
            hello(at(y, z, k // 2, k % 2))

    @pl.when(column_leader)
    def _():
        for k in range(1, NZ):
            hello(at(y, k, 0, 0))

    @pl.when(root)
    def _():
        for k in range(1, NY * NZ):
            hello(at(k // NZ, k % NZ, 0, 0))

    @pl.when(quad != 0)
    def _():
        hello(at(y, z, 0, 0))

    @pl.when(leader & (z != 0))
    def _():
        hello(at(y, 0, 0, 0))

    @pl.when(leader & (place != 0))
    def _():
        hello(at(0, 0, 0, 0))

    leader_peers = 3 + jnp.where(z != 0, 1, NZ - 1) + jnp.where(place != 0, 1, NY * NZ - 1)
    pl.semaphore_wait(barrier, len(everyone) + jnp.where(quad != 0, 1, leader_peers))

    links = Links(send_sems, recv_sems)
    start, need = links.start, links.need

    locals_ = []
    for h in range(STAGES):
        piece = w_ref.at[:, pl.ds(h * 512, 512)]
        mine = G.at[h, y, z, x, c]
        copy = pltpu.make_async_copy(piece, mine, local_sems.at[h])
        copy.start()
        locals_.append(copy)

    kv[0, 2 * SLAB : 3 * SLAB, :] = k_ref[...]
    kv[1, 2 * SLAB : 3 * SLAB, :] = v_ref[...]
    kv[:, 3 * SLAB + 16 :, :] = jnp.zeros((2, SLAB - 16, 512), jnp.bfloat16)
    own_kv = kv.at[:, pl.ds(2 * SLAB, SLAB)]
    first16 = kv.at[:, pl.ds(2 * SLAB, 16)]
    sink_kv = kv.at[:, pl.ds(3 * SLAB, 16)]

    def tree_copy(src, slot, rslot, device):
        return pltpu.make_async_remote_copy(
            src_ref=src, dst_ref=sink_kv, send_sem=tree_send.at[slot], recv_sem=tree_recv.at[rslot],
            device_id=device, device_id_type=MESH)

    def spread(level):
        if level == 0:

            @pl.when(root)
            def _():
                kv[:, 3 * SLAB : 3 * SLAB + 16, :] = kv[:, 2 * SLAB : 2 * SLAB + 16, :]
                for k in range(1, NY):
                    tree_copy(first16, k, 0, at(k, 0, 0, 0)).start()

        if level == 1:

            @pl.when(column_leader & (y != 0))
            def _():
                tree_copy(first16, 0, 0, sib).wait_recv()

            @pl.when(column_leader)
            def _():
                for k in range(1, NZ):
                    tree_copy(sink_kv, 3 + k, 0, at(y, k, 0, 0)).start()

        if level == 2:

            @pl.when(leader & (z != 0))
            def _():
                tree_copy(first16, 0, 0, sib).wait_recv()

            @pl.when(leader)
            def _():
                for k in range(1, 4):
                    tree_copy(sink_kv, 10 + k, 0, at(y, z, k // 2, k % 2)).start()

        if level == 3:

            @pl.when(quad != 0)
            def _():
                tree_copy(first16, 0, 0, sib).wait_recv()

            @pl.when(leader)
            def _():
                for k in range(1, 4):
                    tree_copy(sink_kv, 10 + k, 0, at(y, z, k // 2, k % 2)).wait_send()

            @pl.when(column_leader)
            def _():
                for k in range(1, NZ):
                    tree_copy(sink_kv, 3 + k, 0, at(y, k, 0, 0)).wait_send()

            @pl.when(root)
            def _():
                for k in range(1, NY):
                    tree_copy(first16, k, 0, at(k, 0, 0, 0)).wait_send()

    def lanes(h, first):
        return pl.ds(0, Y_FIRST[h]) if first else pl.ds(Y_FIRST[h], 512 - Y_FIRST[h])

    def block(h, first, ys, zs, xs=pl.ds(0, 2)):
        return G.at[h, ys, zs, xs, c, :, lanes(h, first)]

    one = lambda i: pl.ds(i, 1)
    all_y, all_z = pl.ds(0, NY), pl.ds(0, NZ)
    both = (1, -1)
    ready = set()

    def push(name, ref, device):
        start(name, ref, ref, device)

    def have_x(h):
        if h not in ready:
            ready.add(h)
            locals_[h].wait()
        need(("x", h))

    def halves(h):
        return range(NY) if Y_FIRST[h] == 512 else (None,)

    def last_z(h):
        names = []
        for q in halves(h):
            for d in both:
                if q is None or (q < 2) == (d == 1):
                    names.append(("Az", h, 4, d, q))
        return names

    plus = (0, 1, 2, 3)

    def near():
        start("near", own_kv, kv.at[:, pl.ds(SLAB, SLAB)], after1)

    def far():
        start("far", own_kv, kv.at[:, pl.ds(0, SLAB)], after2)

    def go(i):
        piece = pl.ds(i * 512, 512)
        start(("go", i), go_ref.at[:, piece], go_other.at[:, piece], pair)

    def x_(h):
        start(("x", h), w_ref.at[:, pl.ds(h * 512, 512)], G.at[h, y, z, x, c], x_dev)

    def Ay(h, k):
        have_x(h)
        push(("Ay", h, k), block(h, True, one(y), one(z)), y_dev[k])

    def Az(h, k, d, q):
        if k == 1:
            need(*[("Ay", h, j) for j in (1, -1, 2)])
        else:
            need(("Az", h, k - 1, d, q))
        ys = all_y if q is None else one(q)
        if k == 4 and q is None:
            ys = pl.ds(0 if d == 1 else 2, 2)
        push(("Az", h, k, d, q), block(h, True, ys, one(zm(-d * (k - 1)))), z_dev[d])

    def sA0(h):
        need(*[("Ay", h, j) for j in (1, -1, 2)])
        push(("sA0", h), block(h, True, all_y, one(z)), sib)

    def sAz(h, k, d):
        need(*[("Az", h, k, d, q) for q in halves(h)])
        push(("sAz", h, k, d), block(h, True, all_y, one(zm(-d * k))), sib)

    def sA4(h):
        need(*last_z(h))
        push(("sA4", h), block(h, True, all_y, one(zm(4))), sib)

    def Bz(h, k, d):
        if k == 1:
            have_x(h)
        else:
            need(("Bz", h, k - 1, d))
        xs = pl.ds(0, 2) if k < 4 else one(0 if d == 1 else 1)
        push(("Bz", h, k, d), block(h, False, one(y), one(zm(-d * (k - 1))), xs), z_dev[d])

    def have_z(h, r):
        if r == 0:
            have_x(h)
        elif r == 4:
            need(("Bz", h, 4, 1), ("Bz", h, 4, -1))
        else:
            need(("Bz", h, abs(r), -1 if r > 0 else 1))

    def By(h, d, r):
        have_z(h, r)
        push(("By", h, d, r), block(h, False, one(y), one(zm(r))), y_dev[d])

    def By2(h, d, r):
        need(("By", h, d, r))
        push(("By2", h, d, r), block(h, False, one(ym(-d)), one(zm(r))), y_dev[d])

    def sB0(h):
        for r in range(-3, 5):
            have_z(h, r)
        push(("sB0", h), block(h, False, one(y), all_z), sib)

    def sBy(h, d):
        need(*[("By", h, d, r) for r in range(-3, 5)])
        push(("sBy", h, d), block(h, False, one(ym(-d)), all_z), sib)

    def sB2(h):
        need(*[("By2", h, 1 if r in plus else -1, r) for r in range(-3, 5)])
        push(("sB2", h), block(h, False, one(ym(2)), all_z), sib)

    def gathered(h):
        names = [("sA0", h), ("sA4", h), ("sB0", h), ("sB2", h), ("sBy", h, 1), ("sBy", h, -1)]
        need(*names, *[("sAz", h, k, d) for k in (1, 2, 3) for d in both])

    def masks():
        row = lax.broadcasted_iota(jnp.int32, (SLAB, 4 * SLAB), 0)
        col = lax.broadcasted_iota(jnp.int32, (SLAB, 4 * SLAB), 1)
        first = s * SLAB
        gap = row - col + 2 * SLAB
        band = (col < 3 * SLAB) & (gap >= 0) & (first - 2 * SLAB + col >= SINKS)
        place = col - 3 * SLAB
        sink = (place >= 0) & (place < SINKS) & (place <= first + row)
        dist[...] = jnp.where(band, gap, jnp.where(sink, 0, FAR_AWAY))

    def forward(h):
        need("near", "far")
        keys, vals = kv[0, :, h * HEAD : (h + 1) * HEAD], kv[1, :, h * HEAD : (h + 1) * HEAD]
        for j in range(4 * h, 4 * h + 4):
            cols = slice(j * HEAD, (j + 1) * HEAD)
            scores = dot(q_ref[:, cols], keys, 1, 1)
            scores = jnp.where(dist[...] < win_ref[j], scores, MASKED)
            top = jnp.max(scores, axis=1, keepdims=True)
            p = jnp.exp2((scores - top) * EXP2_SCALE)
            p = p * (1.0 / jnp.sum(p, axis=1, keepdims=True))
            probs[j] = p
            attn[:, cols] = dot(p.astype(jnp.bfloat16), vals, 1, 0).astype(jnp.bfloat16)

    def project(h):
        gathered(h)
        need(*[("go", i) for i in range(4)])
        rows = slice(h * 512, (h + 1) * 512)
        for half in range(2):
            for k in range(4):
                yy, z0 = k // 2, (k % 2) * 4
                w = G[h, 2 * (hd if half == 0 else 1 - hd) + yy, z0 : z0 + 4].reshape(512, 512)
                o = dot(attn[:, rows], w, 1, 1)
                for i in range(4):
                    part = o[:, i * 128 : (i + 1) * 128]
                    acc[half, yy, z0 + i] = part if h == 0 else acc[half, yy, z0 + i] + part
                cols = slice(k * 512, (k + 1) * 512)
                g = dot((go_ref if half == 0 else go_other)[:, cols], w, 1, 0)
                ga[...] = g if half == 0 and k == 0 else ga[...] + g

    def out_lanes(yy, zz):
        return pl.ds(pl.multiple_of(yy * 1024 + zz * 128, 128), 128)

    def project_z(h, k, d):
        if k == 0:
            need(("sA0", h), *[("Ay", h, j) for j in (1, -1, 2)])
        elif k == 4:
            need(("sA4", h), *last_z(h))
        else:
            need(("sAz", h, k, d), *[("Az", h, k, d, q) for q in halves(h)])
        rows = slice(h * 512, (h + 1) * 512)
        zz, n = zm(-d * k), len(sent)
        sent.append(zz)
        for half in (1, 0):
            w = G[h, pl.ds(2 * (hd if half == 0 else 1 - hd), 2), zz].reshape(256, 512)
            o = dot(attn[:, rows], w, 1, 1)
            for yy in range(2):
                part = acc[half, yy, zz] + o[:, yy * 128 : (yy + 1) * 128]
                if half == 1:
                    out_send[n, yy] = part.astype(jnp.bfloat16)
                else:
                    acc[half, yy, zz] = part
            if half == 1:
                start(("out", n), out_send.at[n], out_recv.at[n], pair)
            side = go_ref if half == 0 else go_other
            cols = jnp.concatenate([side[:, out_lanes(0, zz)], side[:, out_lanes(1, zz)]], axis=1)
            g = dot(cols, w, 1, 0)
            ga[...] = g if n == 0 and half == 1 else ga[...] + g

    def backward(h):
        keys, vals = kv[0, :, h * HEAD : (h + 1) * HEAD], kv[1, :, h * HEAD : (h + 1) * HEAD]
        for i in range(4):
            j = 4 * h + i
            cols = slice(j * HEAD, (j + 1) * HEAD)
            g = ga[:, i * HEAD : (i + 1) * HEAD].astype(jnp.bfloat16)
            delta = jnp.sum(
                g.astype(jnp.float32) * attn[:, cols].astype(jnp.float32), axis=1, keepdims=True
            )
            p = probs[j]
            ds = (p * (dot(g, vals, 1, 1) - delta) * SCALE).astype(jnp.bfloat16)
            gq_ref[:, cols] = dot(ds, keys, 1, 0).astype(jnp.bfloat16)
            ds_buf[i * SLAB : (i + 1) * SLAB, :] = ds
            pl_buf[i * SLAB : (i + 1) * SLAB, :] = p.astype(jnp.bfloat16)
        g4 = jnp.concatenate([ga[:, i * HEAD : (i + 1) * HEAD] for i in range(4)], axis=0)
        q4 = jnp.concatenate(
            [q_ref[:, (4 * h + i) * HEAD : (4 * h + i + 1) * HEAD] for i in range(4)], axis=0
        )
        lane = slice(h * HEAD, (h + 1) * HEAD)
        dk = dot(ds_buf[...], q4, 0, 0)
        dv = dot(pl_buf[...], g4.astype(jnp.bfloat16), 0, 0)
        for i, d in enumerate((dk, dv)):
            g_send[h, 0, i] = d[:SLAB].astype(jnp.bfloat16)
            g_send[h, 1, i] = d[SLAB : 2 * SLAB].astype(jnp.bfloat16)
            own[i, :, lane] = d[2 * SLAB : 3 * SLAB]
        upper = lax.broadcasted_iota(jnp.int32, (8, HEAD), 0) < SINKS
        sinks[:, lane] = jnp.where(
            upper, dk[3 * SLAB : 3 * SLAB + 8], pltpu.roll(dv[3 * SLAB : 3 * SLAB + 8], SINKS, 0)
        )
        start(("gfar", h), g_send.at[h, 0], g_recv.at[h, 0], before2)
        start(("gnear", h), g_send.at[h, 1], g_recv.at[h, 1], before1)

    def up(dst, slot, device):
        return pltpu.make_async_remote_copy(
            src_ref=sinks, dst_ref=dst, send_sem=tree_send.at[14], recv_sem=tree_recv.at[1 + slot],
            device_id=device, device_id_type=MESH)

    def collect():
        @pl.when(quad != 0)
        def _():
            copy = up(sink_r1.at[quad - 1], quad - 1, at(y, z, 0, 0))
            copy.start()
            copy.wait_send()

        @pl.when(leader)
        def _():
            for k in range(3):
                up(sink_r1.at[k], k, sib).wait_recv()
            sinks[...] = sinks[...] + sink_r1[0] + sink_r1[1] + sink_r1[2]

            @pl.when(place != 0)
            def _():
                copy = up(sink_r2.at[place - 1], 2 + place, at(0, 0, 0, 0))
                copy.start()
                copy.wait_send()

            @pl.when(place == 0)
            def _():
                total = sinks[...]
                for k in range(NY * NZ - 1):
                    up(sink_r2.at[k], 3 + k, sib).wait_recv()
                    total = total + sink_r2[k]
                keep = lax.broadcasted_iota(jnp.int32, (8, 512), 0) < SINKS
                own[0, 0:8, :] = own[0, 0:8, :] + jnp.where(keep, total, 0.0)
                own[1, 0:8, :] = own[1, 0:8, :] + jnp.where(keep, pltpu.roll(total, SINKS, 0), 0.0)

    sent = []
    act = dict(x=x_, near=near, far=far, go=go, Ay=Ay, Az=Az, sA0=sA0, sAz=sAz, sA4=sA4, Bz=Bz, By=By,
               By2=By2, sB0=sB0, sBy=sBy, sB2=sB2, S=spread, F=forward, PJ=project, PZ=project_z, BW=backward)
    spread(0)
    masks()
    for name, *where in ORDER:
        act[name](*where)
    collect()
    for h in range(STAGES):
        need(("gnear", h), ("gfar", h))
        lane = slice(h * HEAD, (h + 1) * HEAD)
        for i, ref in enumerate((gk_ref, gv_ref)):
            total = own[i, :, lane] + g_recv[h, 0, i].astype(jnp.float32)
            ref[:, lane] = (total + g_recv[h, 1, i].astype(jnp.float32)).astype(jnp.bfloat16)
    for n, zz in enumerate(sent):
        need(("out", n))
        for yy in range(2):
            total = acc[0, yy, zz] + out_recv[n, yy].astype(jnp.float32)
            out_ref[:, out_lanes(yy, zz)] = total.astype(jnp.bfloat16)
    links.finish()


def local(queries, keys, values, windows, out_weight, grad_out):
    vmem = pl.BlockSpec(memory_space=pltpu.VMEM)
    bf, f32 = jnp.bfloat16, jnp.float32
    n_copies = 256
    return pl.pallas_call(
        kernel,
        out_shape=(
            jax.ShapeDtypeStruct((SLAB, 2048), bf),
            jax.ShapeDtypeStruct((SLAB, 2048), bf),
            jax.ShapeDtypeStruct((SLAB, 512), bf),
            jax.ShapeDtypeStruct((SLAB, 512), bf),
        ),
        in_specs=[vmem, vmem, vmem, pl.BlockSpec(memory_space=pltpu.SMEM), vmem, vmem],
        out_specs=(vmem,) * 4,
        scratch_shapes=[
            pltpu.VMEM((STAGES, NY, NZ, 2, 2, 32, 512), bf),
            pltpu.VMEM((2, 4 * SLAB, 512), bf),
            pltpu.VMEM((SLAB, 2048), bf),
            pltpu.VMEM((SLAB, 4 * SLAB), jnp.int32),
            pltpu.VMEM((16, SLAB, 4 * SLAB), f32),
            pltpu.VMEM((SLAB, 2048), bf),
            pltpu.VMEM((SLAB, 512), f32),
            pltpu.VMEM((2, 2, NZ, SLAB, HEAD), f32),
            pltpu.VMEM((NZ, 2, SLAB, HEAD), bf),
            pltpu.VMEM((NZ, 2, SLAB, HEAD), bf),
            pltpu.VMEM((4 * SLAB, 4 * SLAB), bf),
            pltpu.VMEM((4 * SLAB, 4 * SLAB), bf),
            pltpu.VMEM((2, SLAB, 512), f32),
            pltpu.VMEM((STAGES, 2, 2, SLAB, HEAD), bf),
            pltpu.VMEM((STAGES, 2, 2, SLAB, HEAD), bf),
            pltpu.VMEM((8, 512), f32),
            pltpu.VMEM((3, 8, 512), f32),
            pltpu.VMEM((NY * NZ - 1, 8, 512), f32),
            pltpu.SemaphoreType.DMA((n_copies,)),
            pltpu.SemaphoreType.DMA((n_copies,)),
            pltpu.SemaphoreType.DMA((STAGES,)),
            pltpu.SemaphoreType.DMA((15,)),
            pltpu.SemaphoreType.DMA((3 + NY * NZ,)),
        ],
        compiler_params=pltpu.CompilerParams(
            collective_id=0, has_side_effects=True, vmem_limit_bytes=58 << 20
        ),
    )(queries, keys, values, windows, out_weight.T, grad_out)


def solution(mesh):
    cut = P("seq", "head")
    in_specs = (cut, cut, cut, P("head"), P("head", "seq"), cut)
    return jax.shard_map(
        local, mesh=mesh, in_specs=in_specs, out_specs=(cut,) * 4, check_vma=False
    )
```

```python
import functools
import math

import jax
import jax.numpy as jnp
from jax import lax
from jax.experimental import pallas as pl
from jax.experimental.pallas import tpu as pltpu
from jax.sharding import PartitionSpec as P

HEAD = 128
SINKS = 4
SLAB = 128
NY, NZ = 4, 8
MASKED = -1e30
FAR_AWAY = 1 << 20
MESH = pl.DeviceIdType.MESH
SCALE = 1.0 / math.sqrt(HEAD)
EXP2_SCALE = SCALE * math.log2(math.e)
Y_FIRST = (128, 128, 128, 512)
STAGES = 4

ORDER = [
    ("x", 0), ("x", 1), ("x", 2), ("x", 3), ("Ay", 0, 1), ("Ay", 0, -1), ("Ay", 0, 2), ("Bz", 0, 1, 1),
    ("Bz", 0, 1, -1), ("By", 0, 1, 0), ("By", 0, -1, 0), ("Ay", 1, 1), ("Ay", 1, -1), ("Ay", 1, 2),
    ("By", 1, 1, 0), ("By", 1, -1, 0), ("Bz", 1, 1, 1), ("Bz", 1, 1, -1), ("Ay", 2, 1), ("Ay", 2, -1),
    ("Ay", 2, 2), ("By", 2, 1, 0), ("By", 2, -1, 0), ("Bz", 2, 1, 1), ("Bz", 2, 1, -1), ("near",), ("far",),
    ("Ay", 3, 1), ("Ay", 3, -1), ("Ay", 3, 2), ("sA0", 0), ("Az", 0, 1, -1, None), ("Bz", 0, 2, -1),
    ("By", 0, -1, -1), ("Bz", 1, 2, -1), ("sA0", 1), ("Az", 1, 1, -1, None), ("By", 0, -1, 1),
    ("Bz", 2, 2, -1), ("Bz", 0, 2, 1), ("By", 1, -1, -1), ("By2", 0, 1, 0), ("By", 0, 1, 1), ("S", 1),
    ("far2",), ("Az", 0, 1, 1, None), ("sA0", 2), ("By", 1, -1, 1), ("sAz", 0, 1, -1), ("Az", 0, 2, -1, None),
    ("By", 0, 1, -1), ("Az", 2, 1, -1, None), ("By", 2, -1, -1), ("Bz", 1, 2, 1), ("By", 0, 1, 2),
    ("Bz", 0, 3, -1), ("By", 0, -1, 2), ("Az", 1, 1, 1, None), ("go", 0), ("go", 1), ("go", 2),
    ("By2", 1, 1, 0), ("go", 3), ("Bz", 1, 3, -1), ("By", 1, 1, 1), ("By", 1, -1, 2), ("sAz", 1, 1, -1),
    ("Az", 2, 1, 1, None), ("Az", 1, 2, -1, None), ("By2", 0, -1, -1), ("S", 2), ("By", 1, 1, -1), ("sA0", 3),
    ("By", 2, -1, 1), ("Bx", 0, 1, 0), ("Bz", 2, 2, 1), ("By", 1, 1, 2), ("Bz", 2, 3, -1), ("By", 0, -1, -2),
    ("sAz", 0, 2, -1), ("Bz", 0, 3, 1), ("By2", 0, 1, 1), ("Az", 0, 3, -1, None), ("sAz", 0, 1, 1),
    ("By2", 1, -1, -1), ("By", 0, 1, -2), ("Az", 0, 2, 1, None), ("By", 2, -1, 2), ("sAz", 2, 1, -1),
    ("By", 1, 1, -2), ("Az", 2, 2, -1, None), ("By", 1, -1, -2), ("Bz", 1, 3, 1), ("Bx", 1, 1, 0),
    ("By2", 0, 1, 2), ("sAz", 1, 1, 1), ("Bz", 0, 4, -1), ("By", 0, 1, 3), ("By", 0, -1, 3),
    ("Az", 1, 2, 1, None), ("S", 3), ("F", 0), ("Bx", 0, -1, -1), ("By2", 1, 1, 1), ("sAz", 1, 2, -1),
    ("By", 1, 1, 3), ("By", 1, -1, 3), ("Bz", 1, 4, -1), ("Az", 1, 3, -1, None), ("By2", 2, -1, -1),
    ("sAz", 2, 1, 1), ("Az", 2, 2, 1, None), ("Bz", 2, 4, -1), ("By2", 1, 1, 2), ("By", 2, -1, -2),
    ("Bx", 0, 1, 1), ("Az", 3, 1, -1, 0), ("Bz", 2, 3, 1), ("F", 1), ("By2", 0, -1, -2), ("sAz", 0, 2, 1),
    ("sAz", 0, 3, -1), ("Bz", 0, 4, 1), ("By", 0, -1, -3), ("By", 0, 1, -3), ("Az", 0, 3, 1, None),
    ("Az", 0, 4, -1, None), ("Bx", 1, -1, -1), ("By2", 2, 1, 0), ("Bx", 0, 1, 2), ("By2", 1, -1, -2),
    ("By", 1, 1, -3), ("sAz", 2, 2, -1), ("By", 1, -1, -3), ("By", 2, 1, 1), ("Bz", 1, 4, 1),
    ("Az", 2, 3, -1, None), ("F", 2), ("By2", 0, 1, 3), ("Bx", 1, 1, 1), ("sAz", 1, 2, 1), ("sAz", 1, 3, -1),
    ("Az", 1, 3, 1, None), ("Az", 1, 4, -1, None), ("By2", 1, 1, 3), ("Bx", 2, -1, -1), ("By", 2, 1, -1),
    ("By", 2, -1, 3), ("sAz", 2, 2, 1), ("Az", 2, 3, 1, None), ("Bx", 1, 1, 2), ("Az", 3, 1, -1, 1),
    ("Az", 3, 1, -1, 2), ("By", 2, 1, 2), ("F", 3), ("Bx", 0, -1, -2), ("By", 0, -1, 4), ("By", 0, 1, 4),
    ("By2", 0, -1, -3), ("sB0", 0), ("By2", 2, -1, -2), ("Bx", 2, 1, 0), ("By", 2, 1, -2), ("By", 2, -1, -3),
    ("Bx", 1, -1, -2), ("Bz", 2, 4, 1), ("sAz", 0, 3, 1), ("Az", 0, 4, 1, None), ("Az", 3, 1, 1, 0),
    ("Az", 3, 1, -1, 3), ("Az", 3, 2, -1, 0), ("By", 1, -1, 4), ("sB0", 1), ("By", 1, 1, 4),
    ("sAz", 2, 3, -1), ("By2", 1, -1, -3), ("Az", 3, 1, 1, 1), ("Az", 2, 4, -1, None), ("Bx", 0, 1, 3),
    ("By2", 2, 1, 1), ("Az", 3, 1, 1, 2), ("Bx", 1, 1, 3), ("sAz", 1, 3, 1), ("By", 2, 1, 3),
    ("Az", 3, 2, -1, 1), ("By2", 0, -1, 4), ("sBy", 0, -1), ("Az", 1, 4, 1, None), ("sAz", 2, 3, 1),
    ("By", 2, 1, -3), ("Bx", 0, -1, -3), ("By", 2, -1, 4), ("sB0", 2), ("Bx", 2, -1, -2),
    ("Az", 2, 4, 1, None), ("Az", 3, 2, -1, 2), ("By2", 2, 1, 2), ("sA4", 0), ("Az", 3, 1, 1, 3),
    ("By", 2, 1, 4), ("By2", 2, -1, -3), ("sBy", 0, 1), ("sAz", 3, 1, -1), ("Az", 3, 2, -1, 3),
    ("Az", 3, 2, 1, 0), ("By2", 1, -1, 4), ("sBy", 1, -1), ("Bx", 1, -1, -3), ("Az", 3, 3, -1, 0),
    ("Bx", 0, -1, 4), ("sBy", 1, 1), ("Az", 3, 2, 1, 1), ("Bx", 2, 1, 1), ("By2", 2, -1, 4), ("sBy", 2, -1),
    ("Bx", 2, -1, -3), ("By2", 2, 1, 3), ("Az", 3, 2, 1, 2), ("Az", 3, 3, -1, 1), ("Bx", 1, -1, 4),
    ("sB2", 0), ("sA4", 1), ("sA4", 2), ("Az", 3, 3, -1, 2), ("Bx", 2, 1, 2), ("Bx", 2, -1, 4), ("sBy", 2, 1),
    ("sB2", 1), ("sAz", 3, 1, 1), ("sAz", 3, 2, -1), ("Az", 3, 2, 1, 3), ("Az", 3, 3, -1, 3), ("Bx", 2, 1, 3),
    ("PJ", 0), ("Az", 3, 3, 1, 0), ("sB2", 2), ("BW", 0), ("Az", 3, 3, 1, 1), ("PJ", 1), ("Az", 3, 3, 1, 2),
    ("Az", 3, 4, -1, 2), ("sAz", 3, 2, 1), ("sAz", 3, 3, -1), ("Az", 3, 3, 1, 3), ("Az", 3, 4, -1, 3),
    ("PJ", 2), ("Az", 3, 4, 1, 0), ("PZ", 3, 0, 1), ("PZ", 3, 1, 1), ("Az", 3, 4, 1, 1), ("PZ", 3, 1, -1),
    ("PZ", 3, 2, 1), ("PZ", 3, 2, -1), ("PZ", 3, 3, -1), ("BW", 1), ("BW", 2), ("sAz", 3, 3, 1), ("sA4", 3),
    ("PZ", 3, 3, 1), ("PZ", 3, 4, 1), ("BW", 3),
]


def dot(a, b, ca, cb):
    return lax.dot_general(a, b, (((ca,), (cb,)), ((), ())), preferred_element_type=jnp.float32)


class Links:
    def __init__(self, send_sems, recv_sems):
        self.send_sems, self.recv_sems = send_sems, recv_sems
        self.copies, self.arrived = {}, set()

    def start(self, name, src, dst, device):
        n = len(self.copies)
        copy = pltpu.make_async_remote_copy(
            src_ref=src,
            dst_ref=dst,
            send_sem=self.send_sems.at[n],
            recv_sem=self.recv_sems.at[n],
            device_id=device,
            device_id_type=MESH,
        )
        copy.start()
        self.copies[name] = copy

    def need(self, *names):
        for name in names:
            if name not in self.arrived:
                self.arrived.add(name)
                self.copies[name].wait_recv()

    def finish(self):
        self.need(*self.copies)
        for copy in self.copies.values():
            copy.wait_send()


def kernel(
    q_ref, k_ref, v_ref, win_ref, w_ref, go_ref,
    out_ref, gq_ref, gk_ref, gv_ref,
    G, kv, go_other, dist, probs, attn, ga, acc, out_send, out_recv, ds_buf, pl_buf, own, near_own,
    g_send, g_recv, sinks, sink_r1, sink_r2,
    send_sems, recv_sems, local_sems, tree_send, tree_recv, pair_send, pair_recv,
):
    s, hd = lax.axis_index("seq"), lax.axis_index("head")
    c, x, z, y = s % 2, (s // 2) % 2, (s // 4) % NZ, s // (4 * NZ)
    n_seq = 4 * NY * NZ

    def at(y, z, x, c):
        return (((y * NZ + z) * 2 + x) * 2 + c, hd)

    def ym(k):
        return (y + k + NY) % NY

    def zm(k):
        return (z + k + NZ) % NZ

    y_dev = {k: at(ym(k), z, x, c) for k in (1, -1, 2)}
    z_dev = {k: at(y, zm(k), x, c) for k in (1, -1)}
    x_dev, sib, pair = at(y, z, 1 - x, c), at(y, z, x, 1 - c), (s, 1 - hd)
    after1, after2 = ((s + 1) % n_seq, hd), ((s + 2) % n_seq, hd)
    before1, before2 = ((s + n_seq - 1) % n_seq, hd), ((s + n_seq - 2) % n_seq, hd)
    quad = 2 * x + c
    leader = quad == 0
    column_leader = leader & (z == 0)
    place = y * NZ + z
    root = column_leader & (y == 0)

    barrier = pltpu.get_barrier_semaphore()

    def hello(device):
        pl.semaphore_signal(barrier, inc=1, device_id=device, device_id_type=MESH)

    everyone = [y_dev[1], y_dev[-1], y_dev[2], z_dev[1], z_dev[-1], x_dev, sib, pair,
                after1, after2, before1, before2]
    for device in everyone:
        hello(device)

    @pl.when(leader)
    def _():
        for k in range(1, 4):
            hello(at(y, z, k // 2, k % 2))

    @pl.when(column_leader)
    def _():
        for k in range(1, NZ):
            hello(at(y, k, 0, 0))

    @pl.when(root)
    def _():
        for k in range(1, NY * NZ):
            hello(at(k // NZ, k % NZ, 0, 0))

    @pl.when(quad != 0)
    def _():
        hello(at(y, z, 0, 0))

    @pl.when(leader & (z != 0))
    def _():
        hello(at(y, 0, 0, 0))

    @pl.when(leader & (place != 0))
    def _():
        hello(at(0, 0, 0, 0))

    leader_peers = 3 + jnp.where(z != 0, 1, NZ - 1) + jnp.where(place != 0, 1, NY * NZ - 1)
    pl.semaphore_wait(barrier, len(everyone) + jnp.where(quad != 0, 1, leader_peers))

    links = Links(send_sems, recv_sems)
    start, need = links.start, links.need

    locals_ = []
    for h in range(STAGES):
        piece = w_ref.at[:, pl.ds(h * 512, 512)]
        mine = G.at[h, y, z, x, c]
        copy = pltpu.make_async_copy(piece, mine, local_sems.at[h])
        copy.start()
        locals_.append(copy)

    kv[0, 2 * SLAB : 3 * SLAB, :] = k_ref[...]
    kv[1, 2 * SLAB : 3 * SLAB, :] = v_ref[...]
    kv[:, 3 * SLAB + 16 :, :] = jnp.zeros((2, SLAB - 16, 512), jnp.bfloat16)
    own_kv = kv.at[:, pl.ds(2 * SLAB, SLAB)]
    first16 = kv.at[:, pl.ds(2 * SLAB, 16)]
    sink_kv = kv.at[:, pl.ds(3 * SLAB, 16)]
    near_kv, far_kv = kv.at[:, pl.ds(SLAB, SLAB)], kv.at[:, pl.ds(0, SLAB)]

    def tree_copy(src, slot, rslot, device):
        return pltpu.make_async_remote_copy(
            src_ref=src, dst_ref=sink_kv, send_sem=tree_send.at[slot], recv_sem=tree_recv.at[rslot],
            device_id=device, device_id_type=MESH)

    def spread(level):
        if level == 0:

            @pl.when(root)
            def _():
                kv[:, 3 * SLAB : 3 * SLAB + 16, :] = kv[:, 2 * SLAB : 2 * SLAB + 16, :]
                for k in range(1, NY):
                    tree_copy(first16, k, 0, at(k, 0, 0, 0)).start()

        if level == 1:

            @pl.when(column_leader & (y != 0))
            def _():
                tree_copy(first16, 0, 0, sib).wait_recv()

            @pl.when(column_leader)
            def _():
                for k in range(1, NZ):
                    tree_copy(sink_kv, 3 + k, 0, at(y, k, 0, 0)).start()

        if level == 2:

            @pl.when(leader & (z != 0))
            def _():
                tree_copy(first16, 0, 0, sib).wait_recv()

            @pl.when(leader)
            def _():
                for k in range(1, 4):
                    tree_copy(sink_kv, 10 + k, 0, at(y, z, k // 2, k % 2)).start()

        if level == 3:

            @pl.when(quad != 0)
            def _():
                tree_copy(first16, 0, 0, sib).wait_recv()

            @pl.when(leader)
            def _():
                for k in range(1, 4):
                    tree_copy(sink_kv, 10 + k, 0, at(y, z, k // 2, k % 2)).wait_send()

            @pl.when(column_leader)
            def _():
                for k in range(1, NZ):
                    tree_copy(sink_kv, 3 + k, 0, at(y, k, 0, 0)).wait_send()

            @pl.when(root)
            def _():
                for k in range(1, NY):
                    tree_copy(first16, k, 0, at(k, 0, 0, 0)).wait_send()

    def lanes(h, first):
        return pl.ds(0, Y_FIRST[h]) if first else pl.ds(Y_FIRST[h], 512 - Y_FIRST[h])

    def block(h, first, ys, zs, xs=pl.ds(0, 2)):
        return G.at[h, ys, zs, xs, c, :, lanes(h, first)]

    one = lambda i: pl.ds(i, 1)
    all_y, all_z = pl.ds(0, NY), pl.ds(0, NZ)
    both = (1, -1)
    ready = set()

    def push(name, ref, device):
        start(name, ref, ref, device)

    def have_x(h):
        if h not in ready:
            ready.add(h)
            locals_[h].wait()
        need(("x", h))

    def halves(h):
        return range(NY) if Y_FIRST[h] == 512 else (None,)

    def last_z(h):
        names = []
        for q in halves(h):
            for d in both:
                if q is None or (q < 2) == (d == 1):
                    names.append(("Az", h, 4, d, q))
        return names

    plus = (0, 1, 2, 3)

    def near():
        need(("x", STAGES - 1))
        start("near", own_kv, near_kv, after1)

    def far_copy(src, slot, device):
        return pltpu.make_async_remote_copy(
            src_ref=src, dst_ref=far_kv, send_sem=pair_send.at[slot], recv_sem=pair_recv.at[0],
            device_id=device, device_id_type=MESH)

    def far():
        @pl.when(c == 0)
        def _():
            far_copy(own_kv, 0, after2).start()

    def far2():
        need("near")

        @pl.when(c == 0)
        def _():
            far_copy(near_kv, 1, sib).start()

    def have_halo():
        need("near")
        if "far" not in ready:
            ready.add("far")
            far_copy(own_kv, 0, sib).wait_recv()

            @pl.when(c == 0)
            def _():
                far_copy(own_kv, 0, after2).wait_send()
                far_copy(near_kv, 1, sib).wait_send()

    def go(i):
        need("near")
        piece = pl.ds(i * 512, 512)
        start(("go", i), go_ref.at[:, piece], go_other.at[:, piece], pair)

    def x_(h):
        start(("x", h), w_ref.at[:, pl.ds(h * 512, 512)], G.at[h, y, z, x, c], x_dev)

    def Ay(h, k):
        have_x(h)
        push(("Ay", h, k), block(h, True, one(y), one(z)), y_dev[k])

    def Az(h, k, d, q):
        if k == 1:
            need(*[("Ay", h, j) for j in (1, -1, 2)])
        else:
            need(("Az", h, k - 1, d, q))
        ys = all_y if q is None else one(q)
        if k == 4 and q is None:
            ys = pl.ds(0 if d == 1 else 2, 2)
        push(("Az", h, k, d, q), block(h, True, ys, one(zm(-d * (k - 1)))), z_dev[d])

    def sA0(h):
        need(*[("Ay", h, j) for j in (1, -1, 2)])
        push(("sA0", h), block(h, True, all_y, one(z)), sib)

    def sAz(h, k, d):
        need(*[("Az", h, k, d, q) for q in halves(h)])
        push(("sAz", h, k, d), block(h, True, all_y, one(zm(-d * k))), sib)

    def sA4(h):
        need(*last_z(h))
        push(("sA4", h), block(h, True, all_y, one(zm(4))), sib)

    def Bz(h, k, d):
        if k == 1:
            have_x(h)
        else:
            need(("Bz", h, k - 1, d))
        xs = pl.ds(0, 2) if k < 4 else one(0 if d == 1 else 1)
        push(("Bz", h, k, d), block(h, False, one(y), one(zm(-d * (k - 1))), xs), z_dev[d])

    def have_z(h, r):
        if r == 0:
            have_x(h)
        elif r == 4:
            need(("Bz", h, 4, 1), ("Bz", h, 4, -1))
        else:
            need(("Bz", h, abs(r), -1 if r > 0 else 1))

    def By(h, d, r):
        have_z(h, r)
        push(("By", h, d, r), block(h, False, one(y), one(zm(r))), y_dev[d])

    def By2(h, d, r):
        need(("By", h, d, r))
        push(("By2", h, d, r), block(h, False, one(ym(-d)), one(zm(r)), one(x)), y_dev[d])

    def Bx(h, d, r):
        need(("By2", h, d, r))
        push(("Bx", h, d, r), block(h, False, one(ym(2)), one(zm(r)), one(x)), x_dev)

    def sB0(h):
        for r in range(-3, 5):
            have_z(h, r)
        push(("sB0", h), block(h, False, one(y), all_z), sib)

    def sBy(h, d):
        need(*[("By", h, d, r) for r in range(-3, 5)])
        push(("sBy", h, d), block(h, False, one(ym(-d)), all_z), sib)

    def sB2(h):
        for name in ("By2", "Bx"):
            need(*[(name, h, 1 if r in plus else -1, r) for r in range(-3, 5)])
        push(("sB2", h), block(h, False, one(ym(2)), all_z), sib)

    def gathered(h):
        names = [("sA0", h), ("sA4", h), ("sB0", h), ("sB2", h), ("sBy", h, 1), ("sBy", h, -1)]
        need(*names, *[("sAz", h, k, d) for k in (1, 2, 3) for d in both])

    def masks():
        row = lax.broadcasted_iota(jnp.int32, (SLAB, 4 * SLAB), 0)
        col = lax.broadcasted_iota(jnp.int32, (SLAB, 4 * SLAB), 1)
        first = s * SLAB
        gap = row - col + 2 * SLAB
        band = (col < 3 * SLAB) & (gap >= 0) & (first - 2 * SLAB + col >= SINKS)
        place = col - 3 * SLAB
        sink = (place >= 0) & (place < SINKS) & (place <= first + row)
        dist[...] = jnp.where(band, gap, jnp.where(sink, 0, FAR_AWAY))

    def forward(h):
        have_halo()
        keys, vals = kv[0, :, h * HEAD : (h + 1) * HEAD], kv[1, :, h * HEAD : (h + 1) * HEAD]
        for j in range(4 * h, 4 * h + 4):
            cols = slice(j * HEAD, (j + 1) * HEAD)
            scores = dot(q_ref[:, cols], keys, 1, 1)
            scores = jnp.where(dist[...] < win_ref[j], scores, MASKED)
            top = jnp.max(scores, axis=1, keepdims=True)
            p = jnp.exp2((scores - top) * EXP2_SCALE)
            p = p * (1.0 / jnp.sum(p, axis=1, keepdims=True))
            probs[j] = p
            attn[:, cols] = dot(p.astype(jnp.bfloat16), vals, 1, 0).astype(jnp.bfloat16)

    def project(h):
        gathered(h)
        need(*[("go", i) for i in range(4)])
        rows = slice(h * 512, (h + 1) * 512)
        for half in range(2):
            for k in range(4):
                yy, z0 = k // 2, (k % 2) * 4
                w = G[h, 2 * (hd if half == 0 else 1 - hd) + yy, z0 : z0 + 4].reshape(512, 512)
                o = dot(attn[:, rows], w, 1, 1)
                for i in range(4):
                    part = o[:, i * 128 : (i + 1) * 128]
                    acc[half, yy, z0 + i] = part if h == 0 else acc[half, yy, z0 + i] + part
                cols = slice(k * 512, (k + 1) * 512)
                g = dot((go_ref if half == 0 else go_other)[:, cols], w, 1, 0)
                ga[h] = g if half == 0 and k == 0 else ga[h] + g

    def out_lanes(yy, zz):
        return pl.ds(pl.multiple_of(yy * 1024 + zz * 128, 128), 128)

    def project_z(h, k, d):
        if k == 0:
            need(("sA0", h), *[("Ay", h, j) for j in (1, -1, 2)])
        elif k == 4:
            need(("sA4", h), *last_z(h))
        else:
            need(("sAz", h, k, d), *[("Az", h, k, d, q) for q in halves(h)])
        rows = slice(h * 512, (h + 1) * 512)
        zz, n = zm(-d * k), len(sent)
        sent.append(zz)
        for half in (1, 0):
            w = G[h, pl.ds(2 * (hd if half == 0 else 1 - hd), 2), zz].reshape(256, 512)
            o = dot(attn[:, rows], w, 1, 1)
            for yy in range(2):
                part = acc[half, yy, zz] + o[:, yy * 128 : (yy + 1) * 128]
                if half == 1:
                    out_send[n, yy] = part.astype(jnp.bfloat16)
                else:
                    acc[half, yy, zz] = part
            if half == 1:
                start(("out", n), out_send.at[n], out_recv.at[n], pair)
            side = go_ref if half == 0 else go_other
            cols = jnp.concatenate([side[:, out_lanes(0, zz)], side[:, out_lanes(1, zz)]], axis=1)
            g = dot(cols, w, 1, 0)
            ga[h] = g if n == 0 and half == 1 else ga[h] + g

    def backward(h):
        keys, vals = kv[0, :, h * HEAD : (h + 1) * HEAD], kv[1, :, h * HEAD : (h + 1) * HEAD]
        for i in range(4):
            j = 4 * h + i
            cols = slice(j * HEAD, (j + 1) * HEAD)
            g = ga[h, :, i * HEAD : (i + 1) * HEAD].astype(jnp.bfloat16)
            delta = jnp.sum(
                g.astype(jnp.float32) * attn[:, cols].astype(jnp.float32), axis=1, keepdims=True
            )
            p = probs[j]
            ds = (p * (dot(g, vals, 1, 1) - delta) * SCALE).astype(jnp.bfloat16)
            gq_ref[:, cols] = dot(ds, keys, 1, 0).astype(jnp.bfloat16)
            ds_buf[i * SLAB : (i + 1) * SLAB, :] = ds
            pl_buf[i * SLAB : (i + 1) * SLAB, :] = p.astype(jnp.bfloat16)
        g4 = jnp.concatenate([ga[h, :, i * HEAD : (i + 1) * HEAD] for i in range(4)], axis=0)
        q4 = jnp.concatenate(
            [q_ref[:, (4 * h + i) * HEAD : (4 * h + i + 1) * HEAD] for i in range(4)], axis=0
        )
        lane = slice(h * HEAD, (h + 1) * HEAD)
        dk = dot(ds_buf[...], q4, 0, 0)
        dv = dot(pl_buf[...], g4.astype(jnp.bfloat16), 0, 0)
        for i, d in enumerate((dk, dv)):
            g_send[h, 0, i] = d[:SLAB].astype(jnp.bfloat16)
            own[i, :, lane] = d[2 * SLAB : 3 * SLAB]
        upper = lax.broadcasted_iota(jnp.int32, (8, HEAD), 0) < SINKS
        sinks[:, lane] = jnp.where(
            upper, dk[3 * SLAB : 3 * SLAB + 8], pltpu.roll(dv[3 * SLAB : 3 * SLAB + 8], SINKS, 0)
        )
        far_grad(h).start()

        for i, d in enumerate((dk, dv)):
            near_own[h, i] = d[SLAB : 2 * SLAB]

    def send_near(h):
        @pl.when(c == 0)
        def _():
            arrived(h, 1).wait_recv()
            g_send[h, 1] = (near_own[h] + g_recv[h, 2].astype(jnp.float32)).astype(jnp.bfloat16)

        @pl.when(c != 0)
        def _():
            g_send[h, 1] = near_own[h].astype(jnp.bfloat16)

        start(("gnear", h), g_send.at[h, 1], g_recv.at[h, 1], before1)

    far_owner = (jnp.where(c == 0, before2[0], sib[0]), hd)

    def far_grad(h):
        return pltpu.make_async_remote_copy(
            src_ref=g_send.at[h, 0], dst_ref=g_recv.at[h, 2 * c], send_sem=pair_send.at[2 + h],
            recv_sem=pair_recv.at[1 + 2 * h + c], device_id=far_owner, device_id_type=MESH)

    def arrived(h, from_core):
        return pltpu.make_async_remote_copy(
            src_ref=g_send.at[h, 0], dst_ref=g_recv.at[h, 2 * from_core], send_sem=pair_send.at[2 + h],
            recv_sem=pair_recv.at[1 + 2 * h + from_core], device_id=sib, device_id_type=MESH)

    parts = (pl.ds(0, 384), pl.ds(384, 128))

    def up(part, dst, slot, device):
        lane = parts[part]
        return pltpu.make_async_remote_copy(
            src_ref=sinks.at[:, lane], dst_ref=dst.at[:, lane], send_sem=tree_send.at[14 + part],
            recv_sem=tree_recv.at[1 + 34 * part + slot], device_id=device, device_id_type=MESH)

    def collect(part, level):
        lane = slice(384 * part, 384 + 128 * part)
        if level == 0:

            @pl.when(quad != 0)
            def _():
                up(part, sink_r1.at[quad - 1], quad - 1, at(y, z, 0, 0)).start()

        if level == 1:

            @pl.when(leader)
            def _():
                total = sinks[:, lane]
                for k in range(3):
                    up(part, sink_r1.at[k], k, sib).wait_recv()
                    total = total + sink_r1[k, :, lane]
                sinks[:, lane] = total

            @pl.when(leader & (place != 0))
            def _():
                up(part, sink_r2.at[place - 1], 2 + place, at(0, 0, 0, 0)).start()

        if level == 2:

            @pl.when(root)
            def _():
                total = sinks[:, lane]
                for k in range(NY * NZ - 1):
                    up(part, sink_r2.at[k], 3 + k, sib).wait_recv()
                    total = total + sink_r2[k, :, lane]
                keep = lax.broadcasted_iota(jnp.int32, total.shape, 0) < SINKS
                low = jnp.where(keep, pltpu.roll(total, SINKS, 0), 0.0)
                own[0, 0:8, lane] = own[0, 0:8, lane] + jnp.where(keep, total, 0.0)
                own[1, 0:8, lane] = own[1, 0:8, lane] + low

            @pl.when(jnp.logical_not(root))
            def _():
                up(part, sink_r1.at[0], 0, sib).wait_send()

    sent = []
    act = dict(x=x_, near=near, far=far, far2=far2, go=go, Ay=Ay, Az=Az, sA0=sA0, sAz=sAz, sA4=sA4, Bz=Bz, By=By,
               By2=By2, Bx=Bx, sB0=sB0, sBy=sBy, sB2=sB2, S=spread, F=forward, PJ=project, PZ=project_z, BW=backward)
    spread(0)
    masks()
    for name, *where in ORDER:
        if name == "PZ" and where[1] == 4:
            collect(0, 0)
            for h in range(STAGES - 1):
                send_near(h)
            collect(0, 1)
        act[name](*where)
    collect(1, 0)
    send_near(STAGES - 1)
    collect(1, 1)
    collect(0, 2)
    for n, zz in enumerate(sent):
        need(("out", n))
        for yy in range(2):
            total = acc[0, yy, zz] + out_recv[n, yy].astype(jnp.float32)
            out_ref[:, out_lanes(yy, zz)] = total.astype(jnp.bfloat16)
    collect(1, 2)
    for h in range(STAGES):
        need(("gnear", h))
        far_grad(h).wait_send()
        lane = slice(h * HEAD, (h + 1) * HEAD)

        @pl.when(c == 0)
        def _():
            arrived(h, 0).wait_recv()
            for i in range(2):
                own[i, :, lane] = own[i, :, lane] + g_recv[h, 0, i].astype(jnp.float32)

        for i, ref in enumerate((gk_ref, gv_ref)):
            total = own[i, :, lane] + g_recv[h, 1, i].astype(jnp.float32)
            ref[:, lane] = total.astype(jnp.bfloat16)
    links.finish()


def hand_over(*refs):
    for src, dst in zip(refs[:4], refs[4:], strict=True):
        dst[...] = src[...]


def local(queries, keys, values, windows, out_weight, grad_out):
    vmem = pl.BlockSpec(memory_space=pltpu.VMEM)
    bf, f32 = jnp.bfloat16, jnp.float32
    n_copies = 288
    results = pl.pallas_call(
        kernel,
        out_shape=(
            jax.ShapeDtypeStruct((SLAB, 2048), bf),
            jax.ShapeDtypeStruct((SLAB, 2048), bf),
            jax.ShapeDtypeStruct((SLAB, 512), bf),
            jax.ShapeDtypeStruct((SLAB, 512), bf),
        ),
        in_specs=[vmem, vmem, vmem, pl.BlockSpec(memory_space=pltpu.SMEM), vmem, vmem],
        out_specs=(vmem,) * 4,
        scratch_shapes=[
            pltpu.VMEM((STAGES, NY, NZ, 2, 2, 32, 512), bf),
            pltpu.VMEM((2, 4 * SLAB, 512), bf),
            pltpu.VMEM((SLAB, 2048), bf),
            pltpu.VMEM((SLAB, 4 * SLAB), jnp.int32),
            pltpu.VMEM((16, SLAB, 4 * SLAB), f32),
            pltpu.VMEM((SLAB, 2048), bf),
            pltpu.VMEM((STAGES, SLAB, 512), f32),
            pltpu.VMEM((2, 2, NZ, SLAB, HEAD), f32),
            pltpu.VMEM((NZ, 2, SLAB, HEAD), bf),
            pltpu.VMEM((NZ, 2, SLAB, HEAD), bf),
            pltpu.VMEM((4 * SLAB, 4 * SLAB), bf),
            pltpu.VMEM((4 * SLAB, 4 * SLAB), bf),
            pltpu.VMEM((2, SLAB, 512), f32),
            pltpu.VMEM((STAGES, 2, SLAB, HEAD), f32),
            pltpu.VMEM((STAGES, 2, 2, SLAB, HEAD), bf),
            pltpu.VMEM((STAGES, 3, 2, SLAB, HEAD), bf),
            pltpu.VMEM((8, 512), f32),
            pltpu.VMEM((3, 8, 512), f32),
            pltpu.VMEM((NY * NZ - 1, 8, 512), f32),
            pltpu.SemaphoreType.DMA((n_copies,)),
            pltpu.SemaphoreType.DMA((n_copies,)),
            pltpu.SemaphoreType.DMA((STAGES,)),
            pltpu.SemaphoreType.DMA((16,)),
            pltpu.SemaphoreType.DMA((1 + 2 * 34,)),
            pltpu.SemaphoreType.DMA((2 + STAGES,)),
            pltpu.SemaphoreType.DMA((1 + 2 * STAGES,)),
        ],
        compiler_params=pltpu.CompilerParams(
            collective_id=0, has_side_effects=True, vmem_limit_bytes=58 << 20
        ),
    )(queries, keys, values, windows, out_weight.T, grad_out)
    return pl.pallas_call(
        hand_over,
        out_shape=tuple(jax.ShapeDtypeStruct(r.shape, r.dtype) for r in results),
        in_specs=[vmem] * 4,
        out_specs=(vmem,) * 4,
    )(*results)


def solution(mesh):
    cut = P("seq", "head")
    in_specs = (cut, cut, cut, P("head"), P("head", "seq"), cut)
    return jax.shard_map(
        local, mesh=mesh, in_specs=in_specs, out_specs=(cut,) * 4, check_vma=False
    )
```

```python
import functools
import math

import jax
import jax.numpy as jnp
from jax import lax
from jax.experimental import pallas as pl
from jax.experimental.pallas import tpu as pltpu
from jax.sharding import PartitionSpec as P

HEAD = 128
SINKS = 4
SLAB = 128
NY, NZ = 4, 8
MASKED = -1e30
FAR_AWAY = 1 << 20
MESH = pl.DeviceIdType.MESH
SCALE = 1.0 / math.sqrt(HEAD)
EXP2_SCALE = SCALE * math.log2(math.e)
Y_FIRST = (128, 128, 128, 512)
STAGES = 4

ORDER = [
    ("x", 0), ("x", 1), ("x", 2), ("x", 3), ("Ay", 0, 1), ("Ay", 0, -1), ("Ay", 0, 2), ("Bz", 0, 1, 1),
    ("Bz", 0, 1, -1), ("By", 0, 1, 0), ("By", 0, -1, 0), ("Ay", 1, 1), ("Ay", 1, -1), ("Ay", 1, 2),
    ("By", 1, 1, 0), ("By", 1, -1, 0), ("Bz", 1, 1, 1), ("Bz", 1, 1, -1), ("Ay", 2, 1), ("Ay", 2, -1),
    ("Ay", 2, 2), ("By", 2, 1, 0), ("By", 2, -1, 0), ("Bz", 2, 1, 1), ("Bz", 2, 1, -1), ("near",), ("far",),
    ("Ay", 3, 1), ("Ay", 3, -1), ("Ay", 3, 2), ("sA0", 0), ("Az", 0, 1, -1, None), ("Bz", 0, 2, -1),
    ("By", 0, -1, -1), ("Bz", 1, 2, -1), ("sA0", 1), ("Az", 1, 1, -1, None), ("By", 0, -1, 1),
    ("Bz", 2, 2, -1), ("Bz", 0, 2, 1), ("By", 1, -1, -1), ("By2", 0, 1, 0), ("By", 0, 1, 1), ("far2",),
    ("Az", 0, 1, 1, None), ("sA0", 2), ("By", 1, -1, 1), ("sAz", 0, 1, -1), ("Az", 0, 2, -1, None),
    ("By", 0, 1, -1), ("Az", 2, 1, -1, None), ("By", 2, -1, -1), ("Bz", 1, 2, 1), ("By", 0, 1, 2),
    ("Bz", 0, 3, -1), ("By", 0, -1, 2), ("Az", 1, 1, 1, None), ("go", 0), ("go", 1), ("go", 2),
    ("By2", 1, 1, 0), ("go", 3), ("S", 1), ("Bz", 1, 3, -1), ("By", 1, 1, 1), ("By", 1, -1, 2),
    ("sAz", 1, 1, -1), ("Az", 2, 1, 1, None), ("Az", 1, 2, -1, None), ("By2", 0, -1, -1), ("By", 1, 1, -1),
    ("sA0", 3), ("By", 2, -1, 1), ("Bx", 0, 1, 0), ("Bz", 2, 2, 1), ("By", 1, 1, 2), ("Bz", 2, 3, -1),
    ("By", 0, -1, -2), ("sAz", 0, 2, -1), ("Bz", 0, 3, 1), ("By2", 0, 1, 1), ("Az", 0, 3, -1, None),
    ("sAz", 0, 1, 1), ("By2", 1, -1, -1), ("By", 0, 1, -2), ("Az", 0, 2, 1, None), ("By", 2, -1, 2),
    ("sAz", 2, 1, -1), ("By", 1, 1, -2), ("Az", 2, 2, -1, None), ("By", 1, -1, -2), ("Bz", 1, 3, 1),
    ("Bx", 1, 1, 0), ("By2", 0, 1, 2), ("sAz", 1, 1, 1), ("Bz", 0, 4, -1), ("By", 0, 1, 3), ("By", 0, -1, 3),
    ("Az", 1, 2, 1, None), ("Bx", 0, -1, -1), ("By2", 1, 1, 1), ("sAz", 1, 2, -1), ("By", 1, 1, 3),
    ("By", 1, -1, 3), ("Bz", 1, 4, -1), ("Az", 1, 3, -1, None), ("By2", 2, -1, -1), ("sAz", 2, 1, 1),
    ("Az", 2, 2, 1, None), ("Bz", 2, 4, -1), ("By2", 1, 1, 2), ("S", 2), ("By", 2, -1, -2), ("Bx", 0, 1, 1),
    ("Az", 3, 1, -1, 0), ("Bz", 2, 3, 1), ("By2", 0, -1, -2), ("sAz", 0, 2, 1), ("sAz", 0, 3, -1),
    ("Bz", 0, 4, 1), ("By", 0, -1, -3), ("By", 0, 1, -3), ("Az", 0, 3, 1, None), ("Az", 0, 4, -1, None),
    ("Bx", 1, -1, -1), ("By2", 2, 1, 0), ("Bx", 0, 1, 2), ("By2", 1, -1, -2), ("By", 1, 1, -3),
    ("sAz", 2, 2, -1), ("By", 1, -1, -3), ("By", 2, 1, 1), ("Bz", 1, 4, 1), ("Az", 2, 3, -1, None),
    ("By2", 0, 1, 3), ("Bx", 1, 1, 1), ("sAz", 1, 2, 1), ("sAz", 1, 3, -1), ("Az", 1, 3, 1, None),
    ("Az", 1, 4, -1, None), ("By2", 1, 1, 3), ("Bx", 2, -1, -1), ("By", 2, 1, -1), ("By", 2, -1, 3),
    ("sAz", 2, 2, 1), ("Az", 2, 3, 1, None), ("Bx", 1, 1, 2), ("Az", 3, 1, -1, 1), ("Az", 3, 1, -1, 2),
    ("By", 2, 1, 2), ("Bx", 0, -1, -2), ("By", 0, -1, 4), ("S", 3), ("F", 0), ("By", 0, 1, 4),
    ("By2", 0, -1, -3), ("sB0", 0), ("By2", 2, -1, -2), ("Bx", 2, 1, 0), ("By", 2, 1, -2), ("By", 2, -1, -3),
    ("Bx", 1, -1, -2), ("Bz", 2, 4, 1), ("sAz", 0, 3, 1), ("Az", 0, 4, 1, None), ("Az", 3, 1, 1, 0),
    ("Az", 3, 1, -1, 3), ("Az", 3, 2, -1, 0), ("F", 1), ("By", 1, -1, 4), ("sB0", 1), ("By", 1, 1, 4),
    ("sAz", 2, 3, -1), ("By2", 1, -1, -3), ("Az", 3, 1, 1, 1), ("Az", 2, 4, -1, None), ("Bx", 0, 1, 3),
    ("By2", 2, 1, 1), ("Az", 3, 1, 1, 2), ("Bx", 1, 1, 3), ("sAz", 1, 3, 1), ("By", 2, 1, 3),
    ("Az", 3, 2, -1, 1), ("F", 2), ("By2", 0, -1, 4), ("sBy", 0, -1), ("Az", 1, 4, 1, None), ("sAz", 2, 3, 1),
    ("By", 2, 1, -3), ("Bx", 0, -1, -3), ("By", 2, -1, 4), ("sB0", 2), ("Bx", 2, -1, -2),
    ("Az", 2, 4, 1, None), ("Az", 3, 2, -1, 2), ("By2", 2, 1, 2), ("sA4", 0), ("Az", 3, 1, 1, 3), ("F", 3),
    ("By", 2, 1, 4), ("By2", 2, -1, -3), ("sBy", 0, 1), ("sAz", 3, 1, -1), ("Az", 3, 2, -1, 3),
    ("Az", 3, 2, 1, 0), ("By2", 1, -1, 4), ("sBy", 1, -1), ("Bx", 1, -1, -3), ("Az", 3, 3, -1, 0),
    ("Bx", 0, -1, 4), ("sBy", 1, 1), ("Az", 3, 2, 1, 1), ("Bx", 2, 1, 1), ("By2", 2, -1, 4), ("sBy", 2, -1),
    ("Bx", 2, -1, -3), ("By2", 2, 1, 3), ("Az", 3, 2, 1, 2), ("Az", 3, 3, -1, 1), ("Bx", 1, -1, 4),
    ("sB2", 0), ("sA4", 1), ("sA4", 2), ("Az", 3, 3, -1, 2), ("Bx", 2, 1, 2), ("Bx", 2, -1, 4), ("sBy", 2, 1),
    ("sB2", 1), ("sAz", 3, 1, 1), ("sAz", 3, 2, -1), ("Az", 3, 2, 1, 3), ("Az", 3, 3, -1, 3), ("Bx", 2, 1, 3),
    ("PJ", 0), ("Az", 3, 3, 1, 0), ("sB2", 2), ("BW", 0), ("Az", 3, 3, 1, 1), ("PJ", 1), ("Az", 3, 3, 1, 2),
    ("Az", 3, 4, -1, 2), ("sAz", 3, 2, 1), ("sAz", 3, 3, -1), ("Az", 3, 3, 1, 3), ("Az", 3, 4, -1, 3),
    ("PJ", 2), ("Az", 3, 4, 1, 0), ("PZ", 3, 0, 1), ("PZ", 3, 1, 1), ("Az", 3, 4, 1, 1), ("PZ", 3, 1, -1),
    ("PZ", 3, 2, 1), ("PZ", 3, 2, -1), ("PZ", 3, 3, -1), ("BW", 1), ("BW", 2), ("sAz", 3, 3, 1), ("sA4", 3),
    ("PZ", 3, 3, 1), ("PZ", 3, 4, 1), ("BW", 3),
]


def dot(a, b, ca, cb):
    return lax.dot_general(a, b, (((ca,), (cb,)), ((), ())), preferred_element_type=jnp.float32)


class Links:
    def __init__(self, send_sems, recv_sems):
        self.send_sems, self.recv_sems = send_sems, recv_sems
        self.copies, self.arrived = {}, set()

    def start(self, name, src, dst, device):
        n = len(self.copies)
        copy = pltpu.make_async_remote_copy(
            src_ref=src,
            dst_ref=dst,
            send_sem=self.send_sems.at[n],
            recv_sem=self.recv_sems.at[n],
            device_id=device,
            device_id_type=MESH,
        )
        copy.start()
        self.copies[name] = copy

    def need(self, *names):
        for name in names:
            if name not in self.arrived:
                self.arrived.add(name)
                self.copies[name].wait_recv()

    def finish(self):
        self.need(*self.copies)
        for copy in self.copies.values():
            copy.wait_send()


def kernel(
    q_ref, k_ref, v_ref, win_ref, w_ref, go_ref,
    out_ref, gq_ref, gk_ref, gv_ref,
    G, kv, go_other, dist, probs, attn, ga, acc, out_send, out_recv, ds_buf, pl_buf, own, near_own,
    g_send, g_recv, sinks, sink_r1, sink_r2,
    send_sems, recv_sems, local_sems, tree_send, tree_recv, pair_send, pair_recv,
):
    s, hd = lax.axis_index("seq"), lax.axis_index("head")
    c, x, z, y = s % 2, (s // 2) % 2, (s // 4) % NZ, s // (4 * NZ)
    n_seq = 4 * NY * NZ

    def at(y, z, x, c):
        return (((y * NZ + z) * 2 + x) * 2 + c, hd)

    def ym(k):
        return (y + k + NY) % NY

    def zm(k):
        return (z + k + NZ) % NZ

    y_dev = {k: at(ym(k), z, x, c) for k in (1, -1, 2)}
    z_dev = {k: at(y, zm(k), x, c) for k in (1, -1)}
    x_dev, sib, pair = at(y, z, 1 - x, c), at(y, z, x, 1 - c), (s, 1 - hd)
    after1, after2 = ((s + 1) % n_seq, hd), ((s + 2) % n_seq, hd)
    before1, before2 = ((s + n_seq - 1) % n_seq, hd), ((s + n_seq - 2) % n_seq, hd)
    quad = 2 * x + c
    leader = quad == 0
    column_leader = leader & (z == 0)
    place = y * NZ + z
    root = column_leader & (y == 0)

    barrier = pltpu.get_barrier_semaphore()

    def hello(device):
        pl.semaphore_signal(barrier, inc=1, device_id=device, device_id_type=MESH)

    everyone = [y_dev[1], y_dev[-1], y_dev[2], z_dev[1], z_dev[-1], x_dev, sib, pair,
                after1, after2, before1, before2]
    for device in everyone:
        hello(device)

    @pl.when(leader)
    def _():
        for k in range(1, 4):
            hello(at(y, z, k // 2, k % 2))

    @pl.when(column_leader)
    def _():
        for k in range(1, NZ):
            hello(at(y, k, 0, 0))

    @pl.when(root)
    def _():
        for k in range(1, NY * NZ):
            hello(at(k // NZ, k % NZ, 0, 0))

    @pl.when(quad != 0)
    def _():
        hello(at(y, z, 0, 0))

    @pl.when(leader & (z != 0))
    def _():
        hello(at(y, 0, 0, 0))

    @pl.when(leader & (place != 0))
    def _():
        hello(at(0, 0, 0, 0))

    leader_peers = 3 + jnp.where(z != 0, 1, NZ - 1) + jnp.where(place != 0, 1, NY * NZ - 1)
    pl.semaphore_wait(barrier, len(everyone) + jnp.where(quad != 0, 1, leader_peers))

    links = Links(send_sems, recv_sems)
    start, need = links.start, links.need

    locals_ = []
    for h in range(STAGES):
        piece = w_ref.at[:, pl.ds(h * 512, 512)]
        mine = G.at[h, y, z, x, c]
        copy = pltpu.make_async_copy(piece, mine, local_sems.at[h])
        copy.start()
        locals_.append(copy)

    kv[0, 2 * SLAB : 3 * SLAB, :] = k_ref[...]
    kv[1, 2 * SLAB : 3 * SLAB, :] = v_ref[...]
    kv[:, 3 * SLAB + 16 :, :] = jnp.zeros((2, SLAB - 16, 512), jnp.bfloat16)
    own_kv = kv.at[:, pl.ds(2 * SLAB, SLAB)]
    first16 = kv.at[:, pl.ds(2 * SLAB, 16)]
    sink_kv = kv.at[:, pl.ds(3 * SLAB, 16)]
    near_kv, far_kv = kv.at[:, pl.ds(SLAB, SLAB)], kv.at[:, pl.ds(0, SLAB)]

    def tree_copy(src, slot, rslot, device):
        return pltpu.make_async_remote_copy(
            src_ref=src, dst_ref=sink_kv, send_sem=tree_send.at[slot], recv_sem=tree_recv.at[rslot],
            device_id=device, device_id_type=MESH)

    def spread(level):
        if level == 0:

            @pl.when(root)
            def _():
                kv[:, 3 * SLAB : 3 * SLAB + 16, :] = kv[:, 2 * SLAB : 2 * SLAB + 16, :]
                for k in range(1, NY):
                    tree_copy(first16, k, 0, at(k, 0, 0, 0)).start()

        if level == 1:

            @pl.when(column_leader & (y != 0))
            def _():
                tree_copy(first16, 0, 0, sib).wait_recv()

            @pl.when(column_leader)
            def _():
                for k in range(1, NZ):
                    tree_copy(sink_kv, 3 + k, 0, at(y, k, 0, 0)).start()

        if level == 2:

            @pl.when(leader & (z != 0))
            def _():
                tree_copy(first16, 0, 0, sib).wait_recv()

            @pl.when(leader)
            def _():
                for k in range(1, 4):
                    tree_copy(sink_kv, 10 + k, 0, at(y, z, k // 2, k % 2)).start()

        if level == 3:

            @pl.when(quad != 0)
            def _():
                tree_copy(first16, 0, 0, sib).wait_recv()

            @pl.when(leader)
            def _():
                for k in range(1, 4):
                    tree_copy(sink_kv, 10 + k, 0, at(y, z, k // 2, k % 2)).wait_send()

            @pl.when(column_leader)
            def _():
                for k in range(1, NZ):
                    tree_copy(sink_kv, 3 + k, 0, at(y, k, 0, 0)).wait_send()

            @pl.when(root)
            def _():
                for k in range(1, NY):
                    tree_copy(first16, k, 0, at(k, 0, 0, 0)).wait_send()

    def lanes(h, first):
        return pl.ds(0, Y_FIRST[h]) if first else pl.ds(Y_FIRST[h], 512 - Y_FIRST[h])

    def block(h, first, ys, zs, xs=pl.ds(0, 2)):
        return G.at[h, ys, zs, xs, c, :, lanes(h, first)]

    one = lambda i: pl.ds(i, 1)
    all_y, all_z = pl.ds(0, NY), pl.ds(0, NZ)
    both = (1, -1)
    ready = set()

    def push(name, ref, device):
        start(name, ref, ref, device)

    def have_x(h):
        if h not in ready:
            ready.add(h)
            locals_[h].wait()
        need(("x", h))

    def halves(h):
        return range(NY) if Y_FIRST[h] == 512 else (None,)

    def last_z(h):
        names = []
        for q in halves(h):
            for d in both:
                if q is None or (q < 2) == (d == 1):
                    names.append(("Az", h, 4, d, q))
        return names

    plus = (0, 1, 2, 3)

    def near():
        need(("x", STAGES - 1))
        start("near", own_kv, near_kv, after1)

    def far_copy(src, slot, device):
        return pltpu.make_async_remote_copy(
            src_ref=src, dst_ref=far_kv, send_sem=pair_send.at[slot], recv_sem=pair_recv.at[0],
            device_id=device, device_id_type=MESH)

    def far():
        @pl.when(c == 0)
        def _():
            far_copy(own_kv, 0, after2).start()

    def far2():
        need("near")

        @pl.when(c == 0)
        def _():
            far_copy(near_kv, 1, sib).start()

    def have_halo():
        need("near")
        if "far" not in ready:
            ready.add("far")
            far_copy(own_kv, 0, sib).wait_recv()

            @pl.when(c == 0)
            def _():
                far_copy(own_kv, 0, after2).wait_send()
                far_copy(near_kv, 1, sib).wait_send()

    def go(i):
        need("near")
        piece = pl.ds(i * 512, 512)
        start(("go", i), go_ref.at[:, piece], go_other.at[:, piece], pair)

    def x_(h):
        start(("x", h), w_ref.at[:, pl.ds(h * 512, 512)], G.at[h, y, z, x, c], x_dev)

    def Ay(h, k):
        have_x(h)
        push(("Ay", h, k), block(h, True, one(y), one(z)), y_dev[k])

    def Az(h, k, d, q):
        if k == 1:
            need(*[("Ay", h, j) for j in (1, -1, 2)])
        else:
            need(("Az", h, k - 1, d, q))
        ys = all_y if q is None else one(q)
        if k == 4 and q is None:
            ys = pl.ds(0 if d == 1 else 2, 2)
        push(("Az", h, k, d, q), block(h, True, ys, one(zm(-d * (k - 1)))), z_dev[d])

    def sA0(h):
        need(*[("Ay", h, j) for j in (1, -1, 2)])
        push(("sA0", h), block(h, True, all_y, one(z)), sib)

    def sAz(h, k, d):
        need(*[("Az", h, k, d, q) for q in halves(h)])
        push(("sAz", h, k, d), block(h, True, all_y, one(zm(-d * k))), sib)

    def sA4(h):
        need(*last_z(h))
        push(("sA4", h), block(h, True, all_y, one(zm(4))), sib)

    def Bz(h, k, d):
        if k == 1:
            have_x(h)
        else:
            need(("Bz", h, k - 1, d))
        xs = pl.ds(0, 2) if k < 4 else one(0 if d == 1 else 1)
        push(("Bz", h, k, d), block(h, False, one(y), one(zm(-d * (k - 1))), xs), z_dev[d])

    def have_z(h, r):
        if r == 0:
            have_x(h)
        elif r == 4:
            need(("Bz", h, 4, 1), ("Bz", h, 4, -1))
        else:
            need(("Bz", h, abs(r), -1 if r > 0 else 1))

    def By(h, d, r):
        have_z(h, r)
        push(("By", h, d, r), block(h, False, one(y), one(zm(r))), y_dev[d])

    def By2(h, d, r):
        need(("By", h, d, r))
        push(("By2", h, d, r), block(h, False, one(ym(-d)), one(zm(r)), one(x)), y_dev[d])

    def Bx(h, d, r):
        need(("By2", h, d, r))
        push(("Bx", h, d, r), block(h, False, one(ym(2)), one(zm(r)), one(x)), x_dev)

    def sB0(h):
        for r in range(-3, 5):
            have_z(h, r)
        push(("sB0", h), block(h, False, one(y), all_z), sib)

    def sBy(h, d):
        need(*[("By", h, d, r) for r in range(-3, 5)])
        push(("sBy", h, d), block(h, False, one(ym(-d)), all_z), sib)

    def sB2(h):
        for name in ("By2", "Bx"):
            need(*[(name, h, 1 if r in plus else -1, r) for r in range(-3, 5)])
        push(("sB2", h), block(h, False, one(ym(2)), all_z), sib)

    def gathered(h):
        names = [("sA0", h), ("sA4", h), ("sB0", h), ("sB2", h), ("sBy", h, 1), ("sBy", h, -1)]
        need(*names, *[("sAz", h, k, d) for k in (1, 2, 3) for d in both])

    def masks():
        row = lax.broadcasted_iota(jnp.int32, (SLAB, 4 * SLAB), 0)
        col = lax.broadcasted_iota(jnp.int32, (SLAB, 4 * SLAB), 1)
        first = s * SLAB
        gap = row - col + 2 * SLAB
        band = (col < 3 * SLAB) & (gap >= 0) & (first - 2 * SLAB + col >= SINKS)
        place = col - 3 * SLAB
        sink = (place >= 0) & (place < SINKS) & (place <= first + row)
        dist[...] = jnp.where(band, gap, jnp.where(sink, 0, FAR_AWAY))

    def forward(h):
        have_halo()
        keys, vals = kv[0, :, h * HEAD : (h + 1) * HEAD], kv[1, :, h * HEAD : (h + 1) * HEAD]
        for j in range(4 * h, 4 * h + 4):
            cols = slice(j * HEAD, (j + 1) * HEAD)
            scores = dot(q_ref[:, cols], keys, 1, 1)
            scores = jnp.where(dist[...] < win_ref[j], scores, MASKED)
            top = jnp.max(scores, axis=1, keepdims=True)
            p = jnp.exp2((scores - top) * EXP2_SCALE)
            p = p * (1.0 / jnp.sum(p, axis=1, keepdims=True))
            probs[j] = p
            attn[:, cols] = dot(p.astype(jnp.bfloat16), vals, 1, 0).astype(jnp.bfloat16)

    def project(h):
        gathered(h)
        need(*[("go", i) for i in range(4)])
        rows = slice(h * 512, (h + 1) * 512)
        for half in range(2):
            for k in range(4):
                yy, z0 = k // 2, (k % 2) * 4
                w = G[h, 2 * (hd if half == 0 else 1 - hd) + yy, z0 : z0 + 4].reshape(512, 512)
                o = dot(attn[:, rows], w, 1, 1)
                for i in range(4):
                    part = o[:, i * 128 : (i + 1) * 128]
                    acc[half, yy, z0 + i] = part if h == 0 else acc[half, yy, z0 + i] + part
                cols = slice(k * 512, (k + 1) * 512)
                g = dot((go_ref if half == 0 else go_other)[:, cols], w, 1, 0)
                ga[h] = g if half == 0 and k == 0 else ga[h] + g

    def out_lanes(yy, zz):
        return pl.ds(pl.multiple_of(yy * 1024 + zz * 128, 128), 128)

    def project_z(h, k, d):
        if k == 0:
            need(("sA0", h), *[("Ay", h, j) for j in (1, -1, 2)])
        elif k == 4:
            need(("sA4", h), *last_z(h))
        else:
            need(("sAz", h, k, d), *[("Az", h, k, d, q) for q in halves(h)])
        rows = slice(h * 512, (h + 1) * 512)
        zz, n = zm(-d * k), len(sent)
        sent.append(zz)
        for half in (1, 0):
            w = G[h, pl.ds(2 * (hd if half == 0 else 1 - hd), 2), zz].reshape(256, 512)
            o = dot(attn[:, rows], w, 1, 1)
            for yy in range(2):
                part = acc[half, yy, zz] + o[:, yy * 128 : (yy + 1) * 128]
                if half == 1:
                    out_send[n, yy] = part.astype(jnp.bfloat16)
                else:
                    acc[half, yy, zz] = part
            if half == 1:
                start(("out", n), out_send.at[n], out_recv.at[n], pair)
            side = go_ref if half == 0 else go_other
            cols = jnp.concatenate([side[:, out_lanes(0, zz)], side[:, out_lanes(1, zz)]], axis=1)
            g = dot(cols, w, 1, 0)
            ga[h] = g if n == 0 and half == 1 else ga[h] + g

    def backward(h):
        keys, vals = kv[0, :, h * HEAD : (h + 1) * HEAD], kv[1, :, h * HEAD : (h + 1) * HEAD]
        for i in range(4):
            j = 4 * h + i
            cols = slice(j * HEAD, (j + 1) * HEAD)
            g = ga[h, :, i * HEAD : (i + 1) * HEAD].astype(jnp.bfloat16)
            delta = jnp.sum(
                g.astype(jnp.float32) * attn[:, cols].astype(jnp.float32), axis=1, keepdims=True
            )
            p = probs[j]
            ds = (p * (dot(g, vals, 1, 1) - delta) * SCALE).astype(jnp.bfloat16)
            gq_ref[:, cols] = dot(ds, keys, 1, 0).astype(jnp.bfloat16)
            ds_buf[i * SLAB : (i + 1) * SLAB, :] = ds
            pl_buf[i * SLAB : (i + 1) * SLAB, :] = p.astype(jnp.bfloat16)
        g4 = jnp.concatenate([ga[h, :, i * HEAD : (i + 1) * HEAD] for i in range(4)], axis=0)
        q4 = jnp.concatenate(
            [q_ref[:, (4 * h + i) * HEAD : (4 * h + i + 1) * HEAD] for i in range(4)], axis=0
        )
        lane = slice(h * HEAD, (h + 1) * HEAD)
        dk = dot(ds_buf[...], q4, 0, 0)
        dv = dot(pl_buf[...], g4.astype(jnp.bfloat16), 0, 0)
        for i, d in enumerate((dk, dv)):
            g_send[h, 0, i] = d[:SLAB].astype(jnp.bfloat16)
            own[i, :, lane] = d[2 * SLAB : 3 * SLAB]
        upper = lax.broadcasted_iota(jnp.int32, (8, HEAD), 0) < SINKS
        sinks[:, lane] = jnp.where(
            upper, dk[3 * SLAB : 3 * SLAB + 8], pltpu.roll(dv[3 * SLAB : 3 * SLAB + 8], SINKS, 0)
        )
        far_grad(h).start()

        for i, d in enumerate((dk, dv)):
            near_own[h, i] = d[SLAB : 2 * SLAB]

    def send_near(h):
        @pl.when(c == 0)
        def _():
            arrived(h, 1).wait_recv()
            g_send[h, 1] = (near_own[h] + g_recv[h, 2].astype(jnp.float32)).astype(jnp.bfloat16)

        @pl.when(c != 0)
        def _():
            g_send[h, 1] = near_own[h].astype(jnp.bfloat16)

        start(("gnear", h), g_send.at[h, 1], g_recv.at[h, 1], before1)

    far_owner = (jnp.where(c == 0, before2[0], sib[0]), hd)

    def far_grad(h):
        return pltpu.make_async_remote_copy(
            src_ref=g_send.at[h, 0], dst_ref=g_recv.at[h, 2 * c], send_sem=pair_send.at[2 + h],
            recv_sem=pair_recv.at[1 + 2 * h + c], device_id=far_owner, device_id_type=MESH)

    def arrived(h, from_core):
        return pltpu.make_async_remote_copy(
            src_ref=g_send.at[h, 0], dst_ref=g_recv.at[h, 2 * from_core], send_sem=pair_send.at[2 + h],
            recv_sem=pair_recv.at[1 + 2 * h + from_core], device_id=sib, device_id_type=MESH)

    parts = (pl.ds(0, 384), pl.ds(384, 128))

    def up(part, dst, slot, device):
        lane = parts[part]
        return pltpu.make_async_remote_copy(
            src_ref=sinks.at[:, lane], dst_ref=dst.at[:, lane], send_sem=tree_send.at[14 + part],
            recv_sem=tree_recv.at[1 + 34 * part + slot], device_id=device, device_id_type=MESH)

    def collect(part, level):
        lane = slice(384 * part, 384 + 128 * part)
        if level == 0:

            @pl.when(quad != 0)
            def _():
                up(part, sink_r1.at[quad - 1], quad - 1, at(y, z, 0, 0)).start()

        if level == 1:

            @pl.when(leader)
            def _():
                total = sinks[:, lane]
                for k in range(3):
                    up(part, sink_r1.at[k], k, sib).wait_recv()
                    total = total + sink_r1[k, :, lane]
                sinks[:, lane] = total

            @pl.when(leader & (place != 0))
            def _():
                up(part, sink_r2.at[place - 1], 2 + place, at(0, 0, 0, 0)).start()

        if level == 2:

            @pl.when(root)
            def _():
                total = sinks[:, lane]
                for k in range(NY * NZ - 1):
                    up(part, sink_r2.at[k], 3 + k, sib).wait_recv()
                    total = total + sink_r2[k, :, lane]
                keep = lax.broadcasted_iota(jnp.int32, total.shape, 0) < SINKS
                low = jnp.where(keep, pltpu.roll(total, SINKS, 0), 0.0)
                own[0, 0:8, lane] = own[0, 0:8, lane] + jnp.where(keep, total, 0.0)
                own[1, 0:8, lane] = own[1, 0:8, lane] + low

            @pl.when(jnp.logical_not(root))
            def _():
                up(part, sink_r1.at[0], 0, sib).wait_send()

    sent = []
    act = dict(x=x_, near=near, far=far, far2=far2, go=go, Ay=Ay, Az=Az, sA0=sA0, sAz=sAz, sA4=sA4, Bz=Bz, By=By,
               By2=By2, Bx=Bx, sB0=sB0, sBy=sBy, sB2=sB2, S=spread, F=forward, PJ=project, PZ=project_z, BW=backward)
    spread(0)
    masks()
    for name, *where in ORDER:
        if name == "PZ" and where[1] == 4:
            collect(0, 0)
            for h in range(STAGES - 1):
                send_near(h)
            collect(0, 1)
        act[name](*where)
    collect(1, 0)
    send_near(STAGES - 1)
    collect(1, 1)
    collect(0, 2)
    for n, zz in enumerate(sent):
        need(("out", n))
        for yy in range(2):
            total = acc[0, yy, zz] + out_recv[n, yy].astype(jnp.float32)
            out_ref[:, out_lanes(yy, zz)] = total.astype(jnp.bfloat16)
    collect(1, 2)
    for h in range(STAGES):
        need(("gnear", h))
        far_grad(h).wait_send()
        lane = slice(h * HEAD, (h + 1) * HEAD)

        @pl.when(c == 0)
        def _():
            arrived(h, 0).wait_recv()
            for i in range(2):
                own[i, :, lane] = own[i, :, lane] + g_recv[h, 0, i].astype(jnp.float32)

        for i, ref in enumerate((gk_ref, gv_ref)):
            total = own[i, :, lane] + g_recv[h, 1, i].astype(jnp.float32)
            ref[:, lane] = total.astype(jnp.bfloat16)
    links.finish()


def hand_over(*refs):
    for src, dst in zip(refs[:4], refs[4:], strict=True):
        dst[...] = src[...]


def local(queries, keys, values, windows, out_weight, grad_out):
    vmem = pl.BlockSpec(memory_space=pltpu.VMEM)
    bf, f32 = jnp.bfloat16, jnp.float32
    n_copies = 288
    results = pl.pallas_call(
        kernel,
        out_shape=(
            jax.ShapeDtypeStruct((SLAB, 2048), bf),
            jax.ShapeDtypeStruct((SLAB, 2048), bf),
            jax.ShapeDtypeStruct((SLAB, 512), bf),
            jax.ShapeDtypeStruct((SLAB, 512), bf),
        ),
        in_specs=[vmem, vmem, vmem, pl.BlockSpec(memory_space=pltpu.SMEM), vmem, vmem],
        out_specs=(vmem,) * 4,
        scratch_shapes=[
            pltpu.VMEM((STAGES, NY, NZ, 2, 2, 32, 512), bf),
            pltpu.VMEM((2, 4 * SLAB, 512), bf),
            pltpu.VMEM((SLAB, 2048), bf),
            pltpu.VMEM((SLAB, 4 * SLAB), jnp.int32),
            pltpu.VMEM((16, SLAB, 4 * SLAB), f32),
            pltpu.VMEM((SLAB, 2048), bf),
            pltpu.VMEM((STAGES, SLAB, 512), f32),
            pltpu.VMEM((2, 2, NZ, SLAB, HEAD), f32),
            pltpu.VMEM((NZ, 2, SLAB, HEAD), bf),
            pltpu.VMEM((NZ, 2, SLAB, HEAD), bf),
            pltpu.VMEM((4 * SLAB, 4 * SLAB), bf),
            pltpu.VMEM((4 * SLAB, 4 * SLAB), bf),
            pltpu.VMEM((2, SLAB, 512), f32),
            pltpu.VMEM((STAGES, 2, SLAB, HEAD), f32),
            pltpu.VMEM((STAGES, 2, 2, SLAB, HEAD), bf),
            pltpu.VMEM((STAGES, 3, 2, SLAB, HEAD), bf),
            pltpu.VMEM((8, 512), f32),
            pltpu.VMEM((3, 8, 512), f32),
            pltpu.VMEM((NY * NZ - 1, 8, 512), f32),
            pltpu.SemaphoreType.DMA((n_copies,)),
            pltpu.SemaphoreType.DMA((n_copies,)),
            pltpu.SemaphoreType.DMA((STAGES,)),
            pltpu.SemaphoreType.DMA((16,)),
            pltpu.SemaphoreType.DMA((1 + 2 * 34,)),
            pltpu.SemaphoreType.DMA((2 + STAGES,)),
            pltpu.SemaphoreType.DMA((1 + 2 * STAGES,)),
        ],
        compiler_params=pltpu.CompilerParams(
            collective_id=0, has_side_effects=True, vmem_limit_bytes=58 << 20
        ),
    )(queries, keys, values, windows, out_weight.T, grad_out)
    return pl.pallas_call(
        hand_over,
        out_shape=tuple(jax.ShapeDtypeStruct(r.shape, r.dtype) for r in results),
        in_specs=[vmem] * 4,
        out_specs=(vmem,) * 4,
    )(*results)


def solution(mesh):
    cut = P("seq", "head")
    in_specs = (cut, cut, cut, P("head"), P("head", "seq"), cut)
    return jax.shard_map(
        local, mesh=mesh, in_specs=in_specs, out_specs=(cut,) * 4, check_vma=False
    )
```

```python
import functools
import math

import jax
import jax.numpy as jnp
from jax import lax
from jax.experimental import pallas as pl
from jax.experimental.pallas import tpu as pltpu
from jax.sharding import PartitionSpec as P

HEAD = 128
SINKS = 4
SLAB = 128
NY, NZ = 4, 8
MASKED = -1e30
FAR_AWAY = 1 << 20
MESH = pl.DeviceIdType.MESH
SCALE = 1.0 / math.sqrt(HEAD)
EXP2_SCALE = SCALE * math.log2(math.e)
Y_FIRST = (128, 128, 128, 512)
STAGES = 4

ORDER = [
    ("x", 0), ("x", 1), ("x", 2), ("x", 3), ("Ay", 0, 1), ("Ay", 0, -1), ("Ay", 0, 2), ("Bz", 0, 1, 1),
    ("Bz", 0, 1, -1), ("By", 0, 1, 0), ("By", 0, -1, 0), ("Ay", 1, 1), ("Ay", 1, -1), ("Ay", 1, 2),
    ("By", 1, 1, 0), ("By", 1, -1, 0), ("Bz", 1, 1, 1), ("Bz", 1, 1, -1), ("Ay", 2, 1), ("Ay", 2, -1),
    ("Ay", 2, 2), ("By", 2, 1, 0), ("By", 2, -1, 0), ("Bz", 2, 1, 1), ("Bz", 2, 1, -1), ("Ay", 3, 1),
    ("Ay", 3, -1), ("Ay", 3, 2), ("sA0", 0), ("Az", 0, 1, -1, None), ("Bz", 0, 2, -1), ("By", 0, -1, -1),
    ("Bz", 1, 2, -1), ("sA0", 1), ("Az", 1, 1, -1, None), ("By", 0, -1, 1), ("Bz", 2, 2, -1), ("Bz", 0, 2, 1),
    ("By", 1, -1, -1), ("By2", 0, 1, 0), ("By", 0, 1, 1), ("Az", 0, 1, 1, None), ("sA0", 2), ("By", 1, -1, 1),
    ("sAz", 0, 1, -1), ("Az", 0, 2, -1, None), ("By", 0, 1, -1), ("Az", 2, 1, -1, None), ("By", 2, -1, -1),
    ("Bz", 1, 2, 1), ("By", 0, 1, 2), ("Bz", 0, 3, -1), ("By", 0, -1, 2), ("Az", 1, 1, 1, None),
    ("By2", 1, 1, 0), ("near",), ("S", 1), ("far",), ("Bz", 1, 3, -1), ("By", 1, 1, 1), ("By", 1, -1, 2),
    ("sAz", 1, 1, -1), ("Az", 2, 1, 1, None), ("Az", 1, 2, -1, None), ("By2", 0, -1, -1), ("By", 1, 1, -1),
    ("sA0", 3), ("By", 2, -1, 1), ("Bx", 0, 1, 0), ("Bz", 2, 2, 1), ("By", 1, 1, 2), ("Bz", 2, 3, -1),
    ("By", 0, -1, -2), ("sAz", 0, 2, -1), ("Bz", 0, 3, 1), ("By2", 0, 1, 1), ("Az", 0, 3, -1, None),
    ("sAz", 0, 1, 1), ("By2", 1, -1, -1), ("By", 0, 1, -2), ("Az", 0, 2, 1, None), ("By", 2, -1, 2),
    ("sAz", 2, 1, -1), ("By", 1, 1, -2), ("Az", 2, 2, -1, None), ("By", 1, -1, -2), ("Bz", 1, 3, 1),
    ("far2",), ("Bx", 1, 1, 0), ("By2", 0, 1, 2), ("sAz", 1, 1, 1), ("Bz", 0, 4, -1), ("By", 0, 1, 3),
    ("By", 0, -1, 3), ("Az", 1, 2, 1, None), ("Bx", 0, -1, -1), ("By2", 1, 1, 1), ("sAz", 1, 2, -1),
    ("go", 0), ("By", 1, 1, 3), ("By", 1, -1, 3), ("Bz", 1, 4, -1), ("Az", 1, 3, -1, None),
    ("By2", 2, -1, -1), ("sAz", 2, 1, 1), ("Az", 2, 2, 1, None), ("Bz", 2, 4, -1), ("By2", 1, 1, 2), ("S", 2),
    ("go", 1), ("By", 2, -1, -2), ("Bx", 0, 1, 1), ("Az", 3, 1, -1, 0), ("Bz", 2, 3, 1), ("By2", 0, -1, -2),
    ("sAz", 0, 2, 1), ("sAz", 0, 3, -1), ("Bz", 0, 4, 1), ("By", 0, -1, -3), ("By", 0, 1, -3), ("go", 2),
    ("Az", 0, 3, 1, None), ("Az", 0, 4, -1, None), ("Bx", 1, -1, -1), ("By2", 2, 1, 0), ("Bx", 0, 1, 2),
    ("By2", 1, -1, -2), ("By", 1, 1, -3), ("sAz", 2, 2, -1), ("By", 1, -1, -3), ("By", 2, 1, 1), ("go", 3),
    ("Bz", 1, 4, 1), ("Az", 2, 3, -1, None), ("By2", 0, 1, 3), ("Bx", 1, 1, 1), ("sAz", 1, 2, 1),
    ("sAz", 1, 3, -1), ("Az", 1, 3, 1, None), ("Az", 1, 4, -1, None), ("By2", 1, 1, 3), ("Bx", 2, -1, -1),
    ("By", 2, 1, -1), ("By", 2, -1, 3), ("sAz", 2, 2, 1), ("Az", 2, 3, 1, None), ("Bx", 1, 1, 2),
    ("Az", 3, 1, -1, 1), ("Az", 3, 1, -1, 2), ("By", 2, 1, 2), ("Bx", 0, -1, -2), ("By", 0, -1, 4), ("S", 3),
    ("F", 0), ("By", 0, 1, 4), ("By2", 0, -1, -3), ("sB0", 0), ("By2", 2, -1, -2), ("Bx", 2, 1, 0),
    ("By", 2, 1, -2), ("By", 2, -1, -3), ("Bx", 1, -1, -2), ("Bz", 2, 4, 1), ("sAz", 0, 3, 1),
    ("Az", 0, 4, 1, None), ("Az", 3, 1, 1, 0), ("Az", 3, 1, -1, 3), ("Az", 3, 2, -1, 0), ("F", 1),
    ("By", 1, -1, 4), ("sB0", 1), ("By", 1, 1, 4), ("sAz", 2, 3, -1), ("By2", 1, -1, -3), ("Az", 3, 1, 1, 1),
    ("Az", 2, 4, -1, None), ("Bx", 0, 1, 3), ("By2", 2, 1, 1), ("Az", 3, 1, 1, 2), ("Bx", 1, 1, 3),
    ("sAz", 1, 3, 1), ("By", 2, 1, 3), ("Az", 3, 2, -1, 1), ("F", 2), ("By2", 0, -1, 4), ("sBy", 0, -1),
    ("Az", 1, 4, 1, None), ("sAz", 2, 3, 1), ("By", 2, 1, -3), ("Bx", 0, -1, -3), ("By", 2, -1, 4),
    ("sB0", 2), ("Bx", 2, -1, -2), ("Az", 2, 4, 1, None), ("Az", 3, 2, -1, 2), ("By2", 2, 1, 2), ("sA4", 0),
    ("Az", 3, 1, 1, 3), ("F", 3), ("By", 2, 1, 4), ("By2", 2, -1, -3), ("sBy", 0, 1), ("sAz", 3, 1, -1),
    ("Az", 3, 2, -1, 3), ("Az", 3, 2, 1, 0), ("By2", 1, -1, 4), ("sBy", 1, -1), ("Bx", 1, -1, -3),
    ("Az", 3, 3, -1, 0), ("Bx", 0, -1, 4), ("sBy", 1, 1), ("Az", 3, 2, 1, 1), ("Bx", 2, 1, 1),
    ("By2", 2, -1, 4), ("sBy", 2, -1), ("Bx", 2, -1, -3), ("By2", 2, 1, 3), ("Az", 3, 2, 1, 2),
    ("Az", 3, 3, -1, 1), ("Bx", 1, -1, 4), ("sB2", 0), ("sA4", 1), ("sA4", 2), ("Az", 3, 3, -1, 2),
    ("Bx", 2, 1, 2), ("Bx", 2, -1, 4), ("sBy", 2, 1), ("sB2", 1), ("sAz", 3, 1, 1), ("sAz", 3, 2, -1),
    ("Az", 3, 2, 1, 3), ("Az", 3, 3, -1, 3), ("Bx", 2, 1, 3), ("PJ", 0), ("Az", 3, 3, 1, 0), ("sB2", 2),
    ("BW", 0), ("Az", 3, 3, 1, 1), ("PJ", 1), ("Az", 3, 3, 1, 2), ("Az", 3, 4, -1, 2), ("sAz", 3, 2, 1),
    ("sAz", 3, 3, -1), ("Az", 3, 3, 1, 3), ("Az", 3, 4, -1, 3), ("PJ", 2), ("Az", 3, 4, 1, 0),
    ("PZ", 3, 0, 1), ("PZ", 3, 1, 1), ("Az", 3, 4, 1, 1), ("PZ", 3, 1, -1), ("PZ", 3, 2, 1), ("PZ", 3, 2, -1),
    ("PZ", 3, 3, -1), ("BW", 1), ("BW", 2), ("sAz", 3, 3, 1), ("sA4", 3), ("PZ", 3, 3, 1), ("PZ", 3, 4, 1),
    ("BW", 3),
]


def dot(a, b, ca, cb):
    return lax.dot_general(a, b, (((ca,), (cb,)), ((), ())), preferred_element_type=jnp.float32)


class Links:
    def __init__(self, send_sems, recv_sems):
        self.send_sems, self.recv_sems = send_sems, recv_sems
        self.copies, self.arrived = {}, set()

    def start(self, name, src, dst, device):
        n = len(self.copies)
        copy = pltpu.make_async_remote_copy(
            src_ref=src,
            dst_ref=dst,
            send_sem=self.send_sems.at[n],
            recv_sem=self.recv_sems.at[n],
            device_id=device,
            device_id_type=MESH,
        )
        copy.start()
        self.copies[name] = copy

    def need(self, *names):
        for name in names:
            if name not in self.arrived:
                self.arrived.add(name)
                self.copies[name].wait_recv()

    def finish(self):
        self.need(*self.copies)
        for copy in self.copies.values():
            copy.wait_send()


def kernel(
    q_ref, k_ref, v_ref, win_ref, w_ref, go_ref,
    out_ref, gq_ref, gk_ref, gv_ref,
    G, kv, go_other, dist, probs, attn, ga, acc, out_send, out_recv, ds_buf, pl_buf, own, near_own,
    g_send, g_recv, sinks, sink_r1, sink_r2,
    send_sems, recv_sems, local_sems, tree_send, tree_recv, pair_send, pair_recv,
):
    s, hd = lax.axis_index("seq"), lax.axis_index("head")
    c, x, z, y = s % 2, (s // 2) % 2, (s // 4) % NZ, s // (4 * NZ)
    n_seq = 4 * NY * NZ

    def at(y, z, x, c):
        return (((y * NZ + z) * 2 + x) * 2 + c, hd)

    def ym(k):
        return (y + k + NY) % NY

    def zm(k):
        return (z + k + NZ) % NZ

    y_dev = {k: at(ym(k), z, x, c) for k in (1, -1, 2)}
    z_dev = {k: at(y, zm(k), x, c) for k in (1, -1)}
    x_dev, sib, pair = at(y, z, 1 - x, c), at(y, z, x, 1 - c), (s, 1 - hd)
    after1, after2 = ((s + 1) % n_seq, hd), ((s + 2) % n_seq, hd)
    before1, before2 = ((s + n_seq - 1) % n_seq, hd), ((s + n_seq - 2) % n_seq, hd)
    quad = 2 * x + c
    leader = quad == 0
    column_leader = leader & (z == 0)
    place = y * NZ + z
    root = column_leader & (y == 0)

    barrier = pltpu.get_barrier_semaphore()

    def hello(device):
        pl.semaphore_signal(barrier, inc=1, device_id=device, device_id_type=MESH)

    everyone = [y_dev[1], y_dev[-1], y_dev[2], z_dev[1], z_dev[-1], x_dev, sib, pair,
                after1, after2, before1, before2]
    for device in everyone:
        hello(device)

    @pl.when(leader)
    def _():
        for k in range(1, 4):
            hello(at(y, z, k // 2, k % 2))

    @pl.when(column_leader)
    def _():
        for k in range(1, NZ):
            hello(at(y, k, 0, 0))

    @pl.when(root)
    def _():
        for k in range(1, NY * NZ):
            hello(at(k // NZ, k % NZ, 0, 0))

    @pl.when(quad != 0)
    def _():
        hello(at(y, z, 0, 0))

    @pl.when(leader & (z != 0))
    def _():
        hello(at(y, 0, 0, 0))

    @pl.when(leader & (place != 0))
    def _():
        hello(at(0, 0, 0, 0))

    leader_peers = 3 + jnp.where(z != 0, 1, NZ - 1) + jnp.where(place != 0, 1, NY * NZ - 1)
    pl.semaphore_wait(barrier, len(everyone) + jnp.where(quad != 0, 1, leader_peers))

    links = Links(send_sems, recv_sems)
    start, need = links.start, links.need

    locals_ = []
    for h in range(STAGES):
        piece = w_ref.at[:, pl.ds(h * 512, 512)]
        mine = G.at[h, y, z, x, c]
        copy = pltpu.make_async_copy(piece, mine, local_sems.at[h])
        copy.start()
        locals_.append(copy)

    kv[0, 2 * SLAB : 3 * SLAB, :] = k_ref[...]
    kv[1, 2 * SLAB : 3 * SLAB, :] = v_ref[...]
    kv[:, 3 * SLAB + 16 :, :] = jnp.zeros((2, SLAB - 16, 512), jnp.bfloat16)
    own_kv = kv.at[:, pl.ds(2 * SLAB, SLAB)]
    first16 = kv.at[:, pl.ds(2 * SLAB, 16)]
    sink_kv = kv.at[:, pl.ds(3 * SLAB, 16)]
    near_kv, far_kv = kv.at[:, pl.ds(SLAB, SLAB)], kv.at[:, pl.ds(0, SLAB)]

    def tree_copy(src, slot, rslot, device):
        return pltpu.make_async_remote_copy(
            src_ref=src, dst_ref=sink_kv, send_sem=tree_send.at[slot], recv_sem=tree_recv.at[rslot],
            device_id=device, device_id_type=MESH)

    def spread(level):
        if level == 0:

            @pl.when(root)
            def _():
                kv[:, 3 * SLAB : 3 * SLAB + 16, :] = kv[:, 2 * SLAB : 2 * SLAB + 16, :]
                for k in range(1, NY):
                    tree_copy(first16, k, 0, at(k, 0, 0, 0)).start()

        if level == 1:

            @pl.when(column_leader & (y != 0))
            def _():
                tree_copy(first16, 0, 0, sib).wait_recv()

            @pl.when(column_leader)
            def _():
                for k in range(1, NZ):
                    tree_copy(sink_kv, 3 + k, 0, at(y, k, 0, 0)).start()

        if level == 2:

            @pl.when(leader & (z != 0))
            def _():
                tree_copy(first16, 0, 0, sib).wait_recv()

            @pl.when(leader)
            def _():
                for k in range(1, 4):
                    tree_copy(sink_kv, 10 + k, 0, at(y, z, k // 2, k % 2)).start()

        if level == 3:

            @pl.when(quad != 0)
            def _():
                tree_copy(first16, 0, 0, sib).wait_recv()

            @pl.when(leader)
            def _():
                for k in range(1, 4):
                    tree_copy(sink_kv, 10 + k, 0, at(y, z, k // 2, k % 2)).wait_send()

            @pl.when(column_leader)
            def _():
                for k in range(1, NZ):
                    tree_copy(sink_kv, 3 + k, 0, at(y, k, 0, 0)).wait_send()

            @pl.when(root)
            def _():
                for k in range(1, NY):
                    tree_copy(first16, k, 0, at(k, 0, 0, 0)).wait_send()

    def lanes(h, first):
        return pl.ds(0, Y_FIRST[h]) if first else pl.ds(Y_FIRST[h], 512 - Y_FIRST[h])

    def block(h, first, ys, zs, xs=pl.ds(0, 2)):
        return G.at[h, ys, zs, xs, c, :, lanes(h, first)]

    one = lambda i: pl.ds(i, 1)
    all_y, all_z = pl.ds(0, NY), pl.ds(0, NZ)
    both = (1, -1)
    ready = set()

    def push(name, ref, device):
        start(name, ref, ref, device)

    def have_x(h):
        if h not in ready:
            ready.add(h)
            locals_[h].wait()
        need(("x", h))

    def halves(h):
        return range(NY) if Y_FIRST[h] == 512 else (None,)

    def last_z(h):
        names = []
        for q in halves(h):
            for d in both:
                if q is None or (q < 2) == (d == 1):
                    names.append(("Az", h, 4, d, q))
        return names

    plus = (0, 1, 2, 3)

    def near():
        need(("x", STAGES - 1))
        start("near", own_kv, near_kv, after1)

    def far_copy(src, slot, device):
        return pltpu.make_async_remote_copy(
            src_ref=src, dst_ref=far_kv, send_sem=pair_send.at[slot], recv_sem=pair_recv.at[0],
            device_id=device, device_id_type=MESH)

    def far():
        @pl.when(c == 0)
        def _():
            far_copy(own_kv, 0, after2).start()

    def far2():
        need("near")

        @pl.when(c == 0)
        def _():
            far_copy(near_kv, 1, sib).start()

    def have_halo():
        need("near")
        if "far" not in ready:
            ready.add("far")
            far_copy(own_kv, 0, sib).wait_recv()

            @pl.when(c == 0)
            def _():
                far_copy(own_kv, 0, after2).wait_send()
                far_copy(near_kv, 1, sib).wait_send()

    def go(i):
        need("near")
        piece = pl.ds(i * 512, 512)
        start(("go", i), go_ref.at[:, piece], go_other.at[:, piece], pair)

    def x_(h):
        start(("x", h), w_ref.at[:, pl.ds(h * 512, 512)], G.at[h, y, z, x, c], x_dev)

    def Ay(h, k):
        have_x(h)
        push(("Ay", h, k), block(h, True, one(y), one(z)), y_dev[k])

    def Az(h, k, d, q):
        if k == 1:
            need(*[("Ay", h, j) for j in (1, -1, 2)])
        else:
            need(("Az", h, k - 1, d, q))
        ys = all_y if q is None else one(q)
        if k == 4 and q is None:
            ys = pl.ds(0 if d == 1 else 2, 2)
        push(("Az", h, k, d, q), block(h, True, ys, one(zm(-d * (k - 1)))), z_dev[d])

    def sA0(h):
        need(*[("Ay", h, j) for j in (1, -1, 2)])
        push(("sA0", h), block(h, True, all_y, one(z)), sib)

    def sAz(h, k, d):
        need(*[("Az", h, k, d, q) for q in halves(h)])
        push(("sAz", h, k, d), block(h, True, all_y, one(zm(-d * k))), sib)

    def sA4(h):
        need(*last_z(h))
        push(("sA4", h), block(h, True, all_y, one(zm(4))), sib)

    def Bz(h, k, d):
        if k == 1:
            have_x(h)
        else:
            need(("Bz", h, k - 1, d))
        xs = pl.ds(0, 2) if k < 4 else one(0 if d == 1 else 1)
        push(("Bz", h, k, d), block(h, False, one(y), one(zm(-d * (k - 1))), xs), z_dev[d])

    def have_z(h, r):
        if r == 0:
            have_x(h)
        elif r == 4:
            need(("Bz", h, 4, 1), ("Bz", h, 4, -1))
        else:
            need(("Bz", h, abs(r), -1 if r > 0 else 1))

    def By(h, d, r):
        have_z(h, r)
        push(("By", h, d, r), block(h, False, one(y), one(zm(r))), y_dev[d])

    def By2(h, d, r):
        need(("By", h, d, r))
        push(("By2", h, d, r), block(h, False, one(ym(-d)), one(zm(r)), one(x)), y_dev[d])

    def Bx(h, d, r):
        need(("By2", h, d, r))
        push(("Bx", h, d, r), block(h, False, one(ym(2)), one(zm(r)), one(x)), x_dev)

    def sB0(h):
        for r in range(-3, 5):
            have_z(h, r)
        push(("sB0", h), block(h, False, one(y), all_z), sib)

    def sBy(h, d):
        need(*[("By", h, d, r) for r in range(-3, 5)])
        push(("sBy", h, d), block(h, False, one(ym(-d)), all_z), sib)

    def sB2(h):
        for name in ("By2", "Bx"):
            need(*[(name, h, 1 if r in plus else -1, r) for r in range(-3, 5)])
        push(("sB2", h), block(h, False, one(ym(2)), all_z), sib)

    def gathered(h):
        names = [("sA0", h), ("sA4", h), ("sB0", h), ("sB2", h), ("sBy", h, 1), ("sBy", h, -1)]
        need(*names, *[("sAz", h, k, d) for k in (1, 2, 3) for d in both])

    def masks():
        row = lax.broadcasted_iota(jnp.int32, (SLAB, 4 * SLAB), 0)
        col = lax.broadcasted_iota(jnp.int32, (SLAB, 4 * SLAB), 1)
        first = s * SLAB
        gap = row - col + 2 * SLAB
        band = (col < 3 * SLAB) & (gap >= 0) & (first - 2 * SLAB + col >= SINKS)
        place = col - 3 * SLAB
        sink = (place >= 0) & (place < SINKS) & (place <= first + row)
        dist[...] = jnp.where(band, gap, jnp.where(sink, 0, FAR_AWAY))

    def forward(h):
        have_halo()
        keys, vals = kv[0, :, h * HEAD : (h + 1) * HEAD], kv[1, :, h * HEAD : (h + 1) * HEAD]
        for j in range(4 * h, 4 * h + 4):
            cols = slice(j * HEAD, (j + 1) * HEAD)
            scores = dot(q_ref[:, cols], keys, 1, 1)
            scores = jnp.where(dist[...] < win_ref[j], scores, MASKED)
            top = jnp.max(scores, axis=1, keepdims=True)
            p = jnp.exp2((scores - top) * EXP2_SCALE)
            p = p * (1.0 / jnp.sum(p, axis=1, keepdims=True))
            probs[j] = p
            attn[:, cols] = dot(p.astype(jnp.bfloat16), vals, 1, 0).astype(jnp.bfloat16)

    def project(h):
        gathered(h)
        need(*[("go", i) for i in range(4)])
        rows = slice(h * 512, (h + 1) * 512)
        for half in range(2):
            for k in range(4):
                yy, z0 = k // 2, (k % 2) * 4
                w = G[h, 2 * (hd if half == 0 else 1 - hd) + yy, z0 : z0 + 4].reshape(512, 512)
                o = dot(attn[:, rows], w, 1, 1)
                for i in range(4):
                    part = o[:, i * 128 : (i + 1) * 128]
                    acc[half, yy, z0 + i] = part if h == 0 else acc[half, yy, z0 + i] + part
                cols = slice(k * 512, (k + 1) * 512)
                g = dot((go_ref if half == 0 else go_other)[:, cols], w, 1, 0)
                ga[h] = g if half == 0 and k == 0 else ga[h] + g

    def out_lanes(yy, zz):
        return pl.ds(pl.multiple_of(yy * 1024 + zz * 128, 128), 128)

    def project_z(h, k, d):
        if k == 0:
            need(("sA0", h), *[("Ay", h, j) for j in (1, -1, 2)])
        elif k == 4:
            need(("sA4", h), *last_z(h))
        else:
            need(("sAz", h, k, d), *[("Az", h, k, d, q) for q in halves(h)])
        rows = slice(h * 512, (h + 1) * 512)
        zz, n = zm(-d * k), len(sent)
        sent.append(zz)
        for half in (1, 0):
            w = G[h, pl.ds(2 * (hd if half == 0 else 1 - hd), 2), zz].reshape(256, 512)
            o = dot(attn[:, rows], w, 1, 1)
            for yy in range(2):
                part = acc[half, yy, zz] + o[:, yy * 128 : (yy + 1) * 128]
                if half == 1:
                    out_send[n, yy] = part.astype(jnp.bfloat16)
                else:
                    acc[half, yy, zz] = part
            if half == 1:
                start(("out", n), out_send.at[n], out_recv.at[n], pair)
            side = go_ref if half == 0 else go_other
            cols = jnp.concatenate([side[:, out_lanes(0, zz)], side[:, out_lanes(1, zz)]], axis=1)
            g = dot(cols, w, 1, 0)
            ga[h] = g if n == 0 and half == 1 else ga[h] + g

    def backward(h):
        keys, vals = kv[0, :, h * HEAD : (h + 1) * HEAD], kv[1, :, h * HEAD : (h + 1) * HEAD]
        for i in range(4):
            j = 4 * h + i
            cols = slice(j * HEAD, (j + 1) * HEAD)
            g = ga[h, :, i * HEAD : (i + 1) * HEAD].astype(jnp.bfloat16)
            delta = jnp.sum(
                g.astype(jnp.float32) * attn[:, cols].astype(jnp.float32), axis=1, keepdims=True
            )
            p = probs[j]
            ds = (p * (dot(g, vals, 1, 1) - delta) * SCALE).astype(jnp.bfloat16)
            gq_ref[:, cols] = dot(ds, keys, 1, 0).astype(jnp.bfloat16)
            ds_buf[i * SLAB : (i + 1) * SLAB, :] = ds
            pl_buf[i * SLAB : (i + 1) * SLAB, :] = p.astype(jnp.bfloat16)
        g4 = jnp.concatenate([ga[h, :, i * HEAD : (i + 1) * HEAD] for i in range(4)], axis=0)
        q4 = jnp.concatenate(
            [q_ref[:, (4 * h + i) * HEAD : (4 * h + i + 1) * HEAD] for i in range(4)], axis=0
        )
        lane = slice(h * HEAD, (h + 1) * HEAD)
        dk = dot(ds_buf[...], q4, 0, 0)
        dv = dot(pl_buf[...], g4.astype(jnp.bfloat16), 0, 0)
        for i, d in enumerate((dk, dv)):
            g_send[h, 0, i] = d[:SLAB].astype(jnp.bfloat16)
            own[i, :, lane] = d[2 * SLAB : 3 * SLAB]
        upper = lax.broadcasted_iota(jnp.int32, (8, HEAD), 0) < SINKS
        sinks[:, lane] = jnp.where(
            upper, dk[3 * SLAB : 3 * SLAB + 8], pltpu.roll(dv[3 * SLAB : 3 * SLAB + 8], SINKS, 0)
        )
        far_grad(h).start()

        for i, d in enumerate((dk, dv)):
            near_own[h, i] = d[SLAB : 2 * SLAB]

    def send_near(h):
        @pl.when(c == 0)
        def _():
            arrived(h, 1).wait_recv()
            g_send[h, 1] = (near_own[h] + g_recv[h, 2].astype(jnp.float32)).astype(jnp.bfloat16)

        @pl.when(c != 0)
        def _():
            g_send[h, 1] = near_own[h].astype(jnp.bfloat16)

        start(("gnear", h), g_send.at[h, 1], g_recv.at[h, 1], before1)

    far_owner = (jnp.where(c == 0, before2[0], sib[0]), hd)

    def far_grad(h):
        return pltpu.make_async_remote_copy(
            src_ref=g_send.at[h, 0], dst_ref=g_recv.at[h, 2 * c], send_sem=pair_send.at[2 + h],
            recv_sem=pair_recv.at[1 + 2 * h + c], device_id=far_owner, device_id_type=MESH)

    def arrived(h, from_core):
        return pltpu.make_async_remote_copy(
            src_ref=g_send.at[h, 0], dst_ref=g_recv.at[h, 2 * from_core], send_sem=pair_send.at[2 + h],
            recv_sem=pair_recv.at[1 + 2 * h + from_core], device_id=sib, device_id_type=MESH)

    parts = (pl.ds(0, 384), pl.ds(384, 128))

    def up(part, dst, slot, device):
        lane = parts[part]
        return pltpu.make_async_remote_copy(
            src_ref=sinks.at[:, lane], dst_ref=dst.at[:, lane], send_sem=tree_send.at[14 + part],
            recv_sem=tree_recv.at[1 + 34 * part + slot], device_id=device, device_id_type=MESH)

    def collect(part, level):
        lane = slice(384 * part, 384 + 128 * part)
        if level == 0:

            @pl.when(quad != 0)
            def _():
                up(part, sink_r1.at[quad - 1], quad - 1, at(y, z, 0, 0)).start()

        if level == 1:

            @pl.when(leader)
            def _():
                total = sinks[:, lane]
                for k in range(3):
                    up(part, sink_r1.at[k], k, sib).wait_recv()
                    total = total + sink_r1[k, :, lane]
                sinks[:, lane] = total

            @pl.when(leader & (place != 0))
            def _():
                up(part, sink_r2.at[place - 1], 2 + place, at(0, 0, 0, 0)).start()

        if level == 2:

            @pl.when(root)
            def _():
                total = sinks[:, lane]
                for k in range(NY * NZ - 1):
                    up(part, sink_r2.at[k], 3 + k, sib).wait_recv()
                    total = total + sink_r2[k, :, lane]
                keep = lax.broadcasted_iota(jnp.int32, total.shape, 0) < SINKS
                low = jnp.where(keep, pltpu.roll(total, SINKS, 0), 0.0)
                own[0, 0:8, lane] = own[0, 0:8, lane] + jnp.where(keep, total, 0.0)
                own[1, 0:8, lane] = own[1, 0:8, lane] + low

            @pl.when(jnp.logical_not(root))
            def _():
                up(part, sink_r1.at[0], 0, sib).wait_send()

    sent = []
    act = dict(x=x_, near=near, far=far, far2=far2, go=go, Ay=Ay, Az=Az, sA0=sA0, sAz=sAz, sA4=sA4, Bz=Bz, By=By,
               By2=By2, Bx=Bx, sB0=sB0, sBy=sBy, sB2=sB2, S=spread, F=forward, PJ=project, PZ=project_z, BW=backward)
    spread(0)
    masks()
    for name, *where in ORDER:
        if name == "PZ" and where[1] == 4:
            collect(0, 0)
            for h in range(STAGES - 1):
                send_near(h)
            collect(0, 1)
        act[name](*where)
    collect(1, 0)
    send_near(STAGES - 1)
    collect(1, 1)
    collect(0, 2)
    for n, zz in enumerate(sent):
        need(("out", n))
        for yy in range(2):
            total = acc[0, yy, zz] + out_recv[n, yy].astype(jnp.float32)
            out_ref[:, out_lanes(yy, zz)] = total.astype(jnp.bfloat16)
    collect(1, 2)
    for h in range(STAGES):
        need(("gnear", h))
        far_grad(h).wait_send()
        lane = slice(h * HEAD, (h + 1) * HEAD)

        @pl.when(c == 0)
        def _():
            arrived(h, 0).wait_recv()
            for i in range(2):
                own[i, :, lane] = own[i, :, lane] + g_recv[h, 0, i].astype(jnp.float32)

        for i, ref in enumerate((gk_ref, gv_ref)):
            total = own[i, :, lane] + g_recv[h, 1, i].astype(jnp.float32)
            ref[:, lane] = total.astype(jnp.bfloat16)
    links.finish()


def hand_over(*refs):
    for src, dst in zip(refs[:4], refs[4:], strict=True):
        dst[...] = src[...]


def local(queries, keys, values, windows, out_weight, grad_out):
    vmem = pl.BlockSpec(memory_space=pltpu.VMEM)
    bf, f32 = jnp.bfloat16, jnp.float32
    n_copies = 288
    results = pl.pallas_call(
        kernel,
        out_shape=(
            jax.ShapeDtypeStruct((SLAB, 2048), bf),
            jax.ShapeDtypeStruct((SLAB, 2048), bf),
            jax.ShapeDtypeStruct((SLAB, 512), bf),
            jax.ShapeDtypeStruct((SLAB, 512), bf),
        ),
        in_specs=[vmem, vmem, vmem, pl.BlockSpec(memory_space=pltpu.SMEM), vmem, vmem],
        out_specs=(vmem,) * 4,
        scratch_shapes=[
            pltpu.VMEM((STAGES, NY, NZ, 2, 2, 32, 512), bf),
            pltpu.VMEM((2, 4 * SLAB, 512), bf),
            pltpu.VMEM((SLAB, 2048), bf),
            pltpu.VMEM((SLAB, 4 * SLAB), jnp.int32),
            pltpu.VMEM((16, SLAB, 4 * SLAB), f32),
            pltpu.VMEM((SLAB, 2048), bf),
            pltpu.VMEM((STAGES, SLAB, 512), f32),
            pltpu.VMEM((2, 2, NZ, SLAB, HEAD), f32),
            pltpu.VMEM((NZ, 2, SLAB, HEAD), bf),
            pltpu.VMEM((NZ, 2, SLAB, HEAD), bf),
            pltpu.VMEM((4 * SLAB, 4 * SLAB), bf),
            pltpu.VMEM((4 * SLAB, 4 * SLAB), bf),
            pltpu.VMEM((2, SLAB, 512), f32),
            pltpu.VMEM((STAGES, 2, SLAB, HEAD), f32),
            pltpu.VMEM((STAGES, 2, 2, SLAB, HEAD), bf),
            pltpu.VMEM((STAGES, 3, 2, SLAB, HEAD), bf),
            pltpu.VMEM((8, 512), f32),
            pltpu.VMEM((3, 8, 512), f32),
            pltpu.VMEM((NY * NZ - 1, 8, 512), f32),
            pltpu.SemaphoreType.DMA((n_copies,)),
            pltpu.SemaphoreType.DMA((n_copies,)),
            pltpu.SemaphoreType.DMA((STAGES,)),
            pltpu.SemaphoreType.DMA((16,)),
            pltpu.SemaphoreType.DMA((1 + 2 * 34,)),
            pltpu.SemaphoreType.DMA((2 + STAGES,)),
            pltpu.SemaphoreType.DMA((1 + 2 * STAGES,)),
        ],
        compiler_params=pltpu.CompilerParams(
            collective_id=0, has_side_effects=True, vmem_limit_bytes=58 << 20
        ),
    )(queries, keys, values, windows, out_weight.T, grad_out)
    return pl.pallas_call(
        hand_over,
        out_shape=tuple(jax.ShapeDtypeStruct(r.shape, r.dtype) for r in results),
        in_specs=[vmem] * 4,
        out_specs=(vmem,) * 4,
    )(*results)


def solution(mesh):
    cut = P("seq", "head")
    in_specs = (cut, cut, cut, P("head"), P("head", "seq"), cut)
    return jax.shard_map(
        local, mesh=mesh, in_specs=in_specs, out_specs=(cut,) * 4, check_vma=False
    )
```
